512 devices in a mesh: dp: 16 (over x, y_lo, core), fsdp: 32 (over y_hi, z).
Axes of the slice: x: 4, y: 4 (y_hi: 2, y_lo: 2; y = y_hi * 2 + y_lo), z: 16, core: 2. Of those that a mesh axis runs over, the one named last changes fastest.
Arguments:
- hidden: bfloat16 [65536, 8192], P(('dp', 'fsdp')), may hold values from -6 to 6
- queries: bfloat16 [65536, 4096], P(('dp', 'fsdp')), may hold values from -4.5 to 4.5
- keys: bfloat16 [65536, 512], P(('dp', 'fsdp')), may hold values from -4.5 to 4.5
- document_numbers: int32 [16, 4096], P('dp', 'fsdp'), may hold values from 0 to 15, never falling along the last dimension, each value on 1 to 896 neighbouring positions
- adapter_down_weight: bfloat16 [8192, 64], P('fsdp'), may hold values from -0.0625 to 0.0625
- adapter_up_weight: bfloat16 [64, 512], replicated, may hold values from -0.75 to 0.75
- output_gradient: bfloat16 [65536, 4096], P(('dp', 'fsdp')), may hold values from -0.0234375 to 0.0234375
Outputs:
- grad_down: float32 [8192, 64], P('fsdp')
- up_factor_gradient: float32 [64, 512], replicated
The draws below stay inside these ranges and needn't reach their ends.
Inputs may be any that keep to these rules, and one draw needn't show every extreme that they name: `document_numbers`: each document has at most 896 tokens, and some document has exactly 896.
All inputs are finite; a program needn't handle non-finite values.
Results may differ from the reference program's by a relative error of at most 0.0055.
Values may be sent and summed in bfloat16 or wider, within the bound.
No kernel may reach another device: no remote copies, remote signals or barrier semaphores. Data moves between devices by JAX's collectives and lax.ppermute only.
A program may use at most 64 MiB of HBM per device.

```python
import math
import jax
import jax.numpy as jnp
import numpy as np
from jax import lax

MODEL_WIDTH = 8192
QUERY_HEADS = 32
KEY_HEADS = 4
HEAD_SIZE = 128
ADAPTER_RANK = 64
SPAN = 8
SHARD_TOKENS = 128
SEQUENCE_LENGTH = 4096
TOKEN_COUNT = 65536
DOC = 896
NDOCS = 16
N_DP = 16
N_FSDP = 32


def draw_queries(key, part):
    key = jax.random.fold_in(key, 3)
    return jnp.clip(0.3 * jax.random.normal(key, (TOKEN_COUNT, QUERY_HEADS * HEAD_SIZE), jnp.float32), -1.8, 1.8).astype(jnp.bfloat16)


def draw_keys(key, part):
    key = jax.random.fold_in(key, 5)
    return jnp.clip(0.3 * jax.random.normal(key, (TOKEN_COUNT, KEY_HEADS * HEAD_SIZE), jnp.float32), -1.8, 1.8).astype(jnp.bfloat16)


def block_levels(key, extent, cuts, least, top_value):
    loudness, own = 1.0, jax.random.fold_in(key, 6)
    for position, parts in cuts:
        draws = jnp.exp(jax.random.uniform(jax.random.fold_in(own, position), (parts,), jnp.float32, least / len(cuts), top_value / len(cuts)))
        loudness = loudness * jnp.repeat(draws, extent[position] // parts).reshape([-1 if axis == position else 1 for axis in range(len(extent))])
    return loudness


def profile(amount, total, most, skew):
    loads = [(1 << 20) // math.isqrt(grade ** skew) + 1 for grade in range(2, amount + 1)]
    spare, counts = total - most - (amount - 1), [1] * (amount - 1)
    while spare > 0:
        free = [i for i in range(amount - 1) if counts[i] < most]
        pool, remaining = sum([loads[i] for i in free]), spare
        for i in free:
            extra = min(most - counts[i], max(1, remaining * loads[i] // pool), spare)
            counts[i] = counts[i] + extra
            spare = spare - extra
    return np.array([most] + counts)


def uneven(rng, amount, total, most, slope):
    if amount == 2:
        one = jax.random.randint(rng, (), max(1, total - most), min(most, total - 1) + 1)
        return jnp.stack([one, total - one])
    lengths = jnp.asarray(profile(amount, total, most, slope), jnp.int32)
    twos = (amount - 1) // 2
    donor, taker = lengths[1:1 + 2 * twos:2], lengths[2:2 + 2 * twos:2]
    slack = jnp.minimum(donor - 1, most - taker)
    shifted = jax.random.randint(jax.random.fold_in(rng, 1), (twos,), 0, 1 << 20) % (slack + 1)
    lengths = lengths.at[1:1 + 2 * twos:2].set(donor - shifted).at[2:2 + 2 * twos:2].set(taker + shifted)
    return lengths[jax.random.permutation(jax.random.fold_in(rng, 2), amount)]


def gaussian(key, extent, deviation, bound, cuts=(), kind=jnp.bfloat16):
    values = deviation * jax.random.normal(key, extent, jnp.float32)
    if cuts:
        values = values * block_levels(key, extent, cuts, -0.22, 0.18)
    return jnp.clip(values, -bound, bound).astype(kind)


def setup_inputs(seed: int = 0) -> dict:
    key_list = jax.random.split(jax.random.key(seed), 8)
    hidden = gaussian(key_list[0], (TOKEN_COUNT, MODEL_WIDTH), 1.0, 6.0, ((0, 512),))
    queries = draw_queries(jax.random.fold_in(key_list[7], 71), 0)
    keys = draw_keys(jax.random.fold_in(key_list[7], 71), 0)
    document_numbers = jax.vmap(lambda own: jnp.searchsorted(jnp.cumsum(uneven(own, NDOCS, SEQUENCE_LENGTH, DOC, 1)), jnp.arange(SEQUENCE_LENGTH), side="right"))(jax.random.split(key_list[3], N_DP)).reshape((N_DP, SEQUENCE_LENGTH)).astype(jnp.int32)
    adapter_down_weight = gaussian(key_list[4], (MODEL_WIDTH, ADAPTER_RANK), MODEL_WIDTH ** -0.5, 0.0625, ((0, 32),))
    adapter_up_weight = gaussian(key_list[5], (ADAPTER_RANK, KEY_HEADS * HEAD_SIZE), ADAPTER_RANK ** -0.5, 0.75)
    output_gradient = gaussian(key_list[6], (TOKEN_COUNT, QUERY_HEADS * HEAD_SIZE), TOKEN_COUNT ** -0.5, 0.0234375, ((0, 512),))
    return {"hidden": hidden, "queries": queries, "keys": keys, "document_numbers": document_numbers, "adapter_down_weight": adapter_down_weight, "adapter_up_weight": adapter_up_weight, "output_gradient": output_gradient}


def reference(hidden, queries, keys, document_numbers, adapter_down_weight, adapter_up_weight, output_gradient):
    query_group_size = QUERY_HEADS // KEY_HEADS
    key_window = SPAN * SHARD_TOKENS
    leading_rows = (SPAN - 1) * SHARD_TOKENS
    score_scale = 1.0 / math.sqrt(HEAD_SIZE)
    rank_projection = jnp.dot(hidden, adapter_down_weight, preferred_element_type=jnp.float32).astype(jnp.bfloat16)
    head_gradients = output_gradient.reshape(TOKEN_COUNT, KEY_HEADS, query_group_size, HEAD_SIZE)
    up_weight_heads = adapter_up_weight.reshape(ADAPTER_RANK, KEY_HEADS, HEAD_SIZE)
    visible_mask = jnp.einsum('tgmd,rgd->tgmr', head_gradients.astype(jnp.float32), up_weight_heads.astype(jnp.float32)).astype(jnp.bfloat16)

    def single_sequence_step(inputs):
        sequence_query_rows, sequence_key_rows, seq_rank, seq_reached, seq_docs = inputs
        seq_docs = seq_docs.astype(jnp.int32)
        key_rows_padded = jnp.concatenate([jnp.zeros((leading_rows, KEY_HEADS * HEAD_SIZE), sequence_key_rows.dtype), sequence_key_rows], axis=0)
        padded_rank = jnp.concatenate([jnp.zeros((leading_rows, ADAPTER_RANK), seq_rank.dtype), seq_rank], axis=0)
        padded_docs = jnp.concatenate([jnp.full((leading_rows,), -1, jnp.int32), seq_docs], axis=0)

        def block_step(running_totals, block_index):
            start_row_index = (block_index * SHARD_TOKENS).astype(jnp.int32)
            query_block_rows = lax.dynamic_slice_in_dim(sequence_query_rows, start_row_index, SHARD_TOKENS, 0).reshape(SHARD_TOKENS, KEY_HEADS, query_group_size, HEAD_SIZE)
            key_window_rows = lax.dynamic_slice_in_dim(key_rows_padded, start_row_index, key_window, 0).reshape(key_window, KEY_HEADS, HEAD_SIZE)
            window_rank = lax.dynamic_slice_in_dim(padded_rank, start_row_index, key_window, 0)
            window_docs = lax.dynamic_slice_in_dim(padded_docs, start_row_index, key_window, 0)
            query_docs = lax.dynamic_slice_in_dim(seq_docs, start_row_index, SHARD_TOKENS, 0)
            query_pos = start_row_index + jnp.arange(SHARD_TOKENS, dtype=jnp.int32)
            key_pos = start_row_index - leading_rows + jnp.arange(key_window, dtype=jnp.int32)
            visible = (window_docs[None, :] == query_docs[:, None]) & (key_pos[None, :] <= query_pos[:, None])
            scores = jnp.einsum('tgmd,kgd->tgmk', query_block_rows.astype(jnp.float32), key_window_rows.astype(jnp.float32)) * score_scale
            scores = jnp.where(visible[:, None, None, :], scores, -jnp.inf)
            row_max = lax.optimization_barrier(jnp.max(scores, axis=-1, keepdims=True))
            weights = jnp.exp(scores - row_max)
            probs = (weights / lax.optimization_barrier(jnp.sum(weights, axis=-1, keepdims=True))).astype(jnp.bfloat16)
            prob_float = probs.astype(jnp.float32)
            mixed_block = jnp.einsum('tgmk,kr->tgmr', prob_float, window_rank.astype(jnp.float32)).astype(jnp.bfloat16)
            block_reached = lax.dynamic_slice_in_dim(seq_reached, start_row_index, SHARD_TOKENS, 0)
            contrib = jnp.einsum('tgmk,tgmr->kr', prob_float, block_reached.astype(jnp.float32))
            current = lax.dynamic_slice_in_dim(running_totals, start_row_index, key_window, 0)
            running_totals = lax.dynamic_update_slice_in_dim(running_totals, current + contrib, start_row_index, 0)
            return (running_totals, mixed_block)
        start_totals = jnp.zeros((leading_rows + SEQUENCE_LENGTH, ADAPTER_RANK), jnp.float32)
        running_totals, weighted_values = lax.scan(block_step, start_totals, jnp.arange(N_FSDP, dtype=jnp.int32))
        return (running_totals[leading_rows:], weighted_values.reshape(SEQUENCE_LENGTH, KEY_HEADS, query_group_size, ADAPTER_RANK))
    key_partial_sums, weighted_values = lax.map(single_sequence_step, (queries.reshape(N_DP, SEQUENCE_LENGTH, QUERY_HEADS * HEAD_SIZE), keys.reshape(N_DP, SEQUENCE_LENGTH, KEY_HEADS * HEAD_SIZE), rank_projection.reshape(N_DP, SEQUENCE_LENGTH, ADAPTER_RANK), visible_mask.reshape(N_DP, SEQUENCE_LENGTH, KEY_HEADS, query_group_size, ADAPTER_RANK), document_numbers))
    key_grad = key_partial_sums.reshape(TOKEN_COUNT, ADAPTER_RANK).astype(jnp.bfloat16)
    grad_down = jnp.dot(hidden.T, key_grad, preferred_element_type=jnp.float32)
    weighted_values_total = weighted_values.reshape(TOKEN_COUNT, KEY_HEADS, query_group_size, ADAPTER_RANK).astype(jnp.float32)
    up_factor_gradient = jnp.einsum('fsbj,fsbc->jsc', weighted_values_total, head_gradients.astype(jnp.float32)).reshape(ADAPTER_RANK, KEY_HEADS * HEAD_SIZE)
    return (grad_down, up_factor_gradient)
```

```python
import math

import jax
import jax.numpy as jnp
from jax import lax
from jax.experimental import pallas as pl
from jax.experimental.pallas import tpu as pltpu
from jax.sharding import PartitionSpec as P

QUERY_HEADS = 32
KEY_HEADS = 4
HEAD_SIZE = 128
ADAPTER_RANK = 64
SPAN = 8
TOKENS = 128
WINDOW = SPAN * TOKENS
N_DP = 16
N_FSDP = 32
MODEL_WIDTH = 8192
PAIRS = QUERY_HEADS // 2
VMEM_LIMIT = 48 * 1024 * 1024
BF16 = jnp.bfloat16
F32 = jnp.float32
NT = (((1,), (1,)), ((), ()))


def whole(*arrays):
    return [pl.BlockSpec(memory_space=pltpu.VMEM) for _ in arrays]


def params():
    return pltpu.CompilerParams(vmem_limit_bytes=VMEM_LIMIT)


def from_behind(block, distance):
    route = [(i, i + distance) for i in range(N_FSDP) if 0 <= i + distance < N_FSDP]
    return lax.ppermute(block, "fsdp", route)


def exchange(slots, axis):
    return lax.all_to_all(slots, axis, 0, 0, tiled=True)


def after(value, *others):
    return lax.optimization_barrier((value, *others))[0]


def lowrank_kernel(weight_ref, hidden_ref, out_ref):
    total = jnp.zeros((ADAPTER_RANK, TOKENS), F32)
    for f in range(N_FSDP):
        rows = jnp.concatenate(
            [weight_ref[half, :, f * 128 : f * 128 + 128] for half in range(2)], axis=1
        )
        total += lax.dot_general(
            rows, hidden_ref[:, f * 256 : f * 256 + 256], NT, preferred_element_type=F32
        )
    out_ref[...] = total.astype(BF16)


def attention_kernel(
    query_ref,
    gradient_ref,
    up_ref,
    keys3_ref,
    keys2_ref,
    keys1_ref,
    keys0_ref,
    bias_ref,
    probs_ref,
    contrib_ref,
    scores_ref,
    sums_ref,
):
    step = pl.program_id(0)
    factor = math.log2(math.e) / math.sqrt(HEAD_SIZE)
    queries = jnp.concatenate([query_ref[:, :128], query_ref[:, 128:]], axis=0)
    top = jnp.full((1, 256), -jnp.inf, F32)
    key_refs = (keys3_ref, keys2_ref, keys1_ref, keys0_ref)
    for b in range(SPAN):
        keys = key_refs[b // 2][(b % 2) * 128 : (b % 2) * 128 + 128, :]
        rows = slice(b * 128, b * 128 + 128)
        bias = bias_ref[rows, :]
        scores = lax.dot_general(keys, queries, NT, preferred_element_type=F32)
        scores = scores + jnp.concatenate([bias, bias], axis=1)
        scores_ref[rows, :] = scores
        top = jnp.maximum(top, jnp.max(scores, axis=0, keepdims=True))
    shift = top * factor
    total = jnp.zeros((1, 256), F32)
    for b in range(SPAN):
        rows = slice(b * 128, b * 128 + 128)
        weights = jnp.exp2(scores_ref[rows, :] * factor - shift)
        scores_ref[rows, :] = weights
        total += jnp.sum(weights, axis=0, keepdims=True)
    inverse = 1.0 / total
    reached = [
        lax.dot_general(
            gradient_ref[:, half * 128 : half * 128 + 128],
            up_ref[...],
            NT,
            preferred_element_type=F32,
        ).astype(BF16)
        for half in range(2)
    ]
    reached = jnp.concatenate(reached, axis=0)

    @pl.when(step == 0)
    def _():
        sums_ref[...] = jnp.zeros_like(sums_ref)

    for b in range(SPAN):
        rows = slice(b * 128, b * 128 + 128)
        probs = (scores_ref[rows, :] * inverse).astype(BF16)
        probs_ref[rows, :] = probs
        sums_ref[rows, :] += jnp.dot(probs, reached, preferred_element_type=F32)

    @pl.when(step == PAIRS - 1)
    def _():
        contrib_ref[...] = sums_ref[...].T


def attention(queries, gradients, up_weight, key_pairs, bias):
    pair = pl.BlockSpec((TOKENS, 256), lambda p: (0, p))
    keys = pl.BlockSpec((2 * TOKENS, HEAD_SIZE), lambda p: (0, p // 4))
    return pl.pallas_call(
        attention_kernel,
        grid=(PAIRS,),
        in_specs=[
            pair,
            pair,
            pl.BlockSpec((ADAPTER_RANK, HEAD_SIZE), lambda p: (0, p // 4)),
            keys,
            keys,
            keys,
            keys,
            pl.BlockSpec((WINDOW, TOKENS), lambda p: (0, 0)),
        ],
        out_specs=[
            pl.BlockSpec((WINDOW, 256), lambda p: (0, p)),
            pl.BlockSpec((ADAPTER_RANK, WINDOW), lambda p: (0, 0)),
        ],
        out_shape=[
            jax.ShapeDtypeStruct((WINDOW, QUERY_HEADS * TOKENS), BF16),
            jax.ShapeDtypeStruct((ADAPTER_RANK, WINDOW), F32),
        ],
        scratch_shapes=[pltpu.VMEM((WINDOW, 256), F32), pltpu.VMEM((WINDOW, ADAPTER_RANK), F32)],
        compiler_params=params(),
        cost_estimate=pl.CostEstimate(
            flops=3 * 10**9, bytes_accessed=12 * 2**20, transcendentals=4 * 2**20
        ),
        name="attention",
    )(queries, gradients, up_weight, *key_pairs, bias)


def mixed_kernel(probs_ref, rank_ref, gradient_ref, out_ref):
    step = pl.program_id(0)
    mixed = jnp.dot(rank_ref[...], probs_ref[...], preferred_element_type=F32).astype(BF16)
    gradients = jnp.concatenate([gradient_ref[:, :128], gradient_ref[:, 128:]], axis=0)
    share = jnp.dot(mixed, gradients, preferred_element_type=F32)

    @pl.when(step % 4 == 0)
    def _():
        out_ref[...] = share

    @pl.when(step % 4 != 0)
    def _():
        out_ref[...] += share


def mixed_share(probs, rank_window, gradients):
    return pl.pallas_call(
        mixed_kernel,
        grid=(PAIRS,),
        in_specs=[
            pl.BlockSpec((WINDOW, 256), lambda p: (0, p)),
            pl.BlockSpec((ADAPTER_RANK, WINDOW), lambda p: (0, 0)),
            pl.BlockSpec((TOKENS, 256), lambda p: (0, p)),
        ],
        out_specs=pl.BlockSpec((ADAPTER_RANK, HEAD_SIZE), lambda p: (0, p // 4)),
        out_shape=jax.ShapeDtypeStruct((ADAPTER_RANK, KEY_HEADS * HEAD_SIZE), F32),
        compiler_params=params(),
        cost_estimate=pl.CostEstimate(
            flops=6 * 10**8, bytes_accessed=10 * 2**20, transcendentals=0
        ),
        name="mixed",
    )(probs, rank_window, gradients)


DOWN = N_FSDP * 128
LANES = DOWN + 256


def shares_kernel(key_ref, hidden_ref, up_ref, out_ref):
    for f in range(N_FSDP):
        product = jnp.dot(
            key_ref[...], hidden_ref[:, f * 256 : f * 256 + 256], preferred_element_type=F32
        ).astype(BF16)
        for half in range(2):
            out_ref[half, :, f * 128 : f * 128 + 128] = product[:, half * 128 : half * 128 + 128]
    for half in range(2):
        out_ref[half, :, DOWN:] = up_ref[:, half * 256 : half * 256 + 256].astype(BF16)


def fold_dp_kernel(in_ref, out_ref):
    def total(columns):
        return sum(in_ref[d, :, columns].astype(F32) for d in range(N_DP))

    up = total(slice(DOWN, LANES))
    for f in range(N_FSDP):
        out_ref[f, :, :128] = total(slice(f * 128, f * 128 + 128))
        out_ref[f, :, 128:] = up


def fold_fsdp_kernel(in_ref, out_ref):
    total = sum(in_ref[f] for f in range(N_FSDP))
    for d in range(N_DP):
        out_ref[d] = total


def spread_kernel(in_ref, down_ref, up_ref):
    for half in range(2):
        for part in range(8):
            rows = slice(part * 8, part * 8 + 8)
            block = in_ref[half * 8 + part]
            down_ref[rows, half * 128 : half * 128 + 128] = block[:, :128]
            up_ref[rows, half * 256 : half * 256 + 256] = block[:, 128:]


def plain(kernel, name, out_shape, *arrays):
    return pl.pallas_call(
        kernel,
        in_specs=whole(*arrays),
        out_specs=jax.tree.map(lambda _: pl.BlockSpec(memory_space=pltpu.VMEM), out_shape),
        out_shape=out_shape,
        compiler_params=params(),
        name=name,
    )(*arrays)


def local(
    hidden, queries, keys, document_numbers, adapter_down_weight, adapter_up_weight, output_gradient
):
    position = lax.axis_index("fsdp")
    member = lax.axis_index("dp")
    half, part = member // 8, member % 8

    behind_one = from_behind(keys, 1)
    key_pairs = [jnp.concatenate([behind_one, keys], axis=0)]
    weight_slice = lax.dynamic_slice(
        adapter_down_weight.T, (part * 8, half * 128), (8, 128)
    )
    docs_row = document_numbers.reshape(1, TOKENS).astype(BF16)
    slot = jnp.concatenate([weight_slice, docs_row, jnp.zeros((7, 128), BF16)], axis=0)
    slots = jnp.broadcast_to(slot[None], (N_FSDP, 16, 128))
    slots, pair = lax.optimization_barrier((slots, key_pairs[0]))
    key_pairs = [pair]
    key_pairs.insert(0, from_behind(key_pairs[0], 2))
    row_parts = exchange(slots, "fsdp")
    weight_part = row_parts[:, :8].transpose(1, 0, 2).reshape(1, 8, DOWN)
    docs = row_parts[:, 8].astype(jnp.int32)
    weight_slots = jnp.broadcast_to(weight_part, (N_DP, 8, DOWN))
    weight_slots, pair = lax.optimization_barrier((weight_slots, key_pairs[0]))
    key_pairs[0] = pair
    key_pairs.insert(0, from_behind(key_pairs[0], 2))
    weight = exchange(weight_slots, "dp").reshape(2, ADAPTER_RANK, DOWN)
    key_pairs.insert(0, from_behind(key_pairs[0], 2))

    rank = plain(
        lowrank_kernel, "lowrank", jax.ShapeDtypeStruct((ADAPTER_RANK, TOKENS), BF16), weight, hidden
    )
    rank_window = rank
    for distance in (1, 2, 4):
        rank_window = jnp.concatenate([from_behind(rank_window, distance), rank_window], axis=1)

    padded = jnp.concatenate([jnp.full((SPAN - 1, TOKENS), -1, jnp.int32), docs], axis=0)
    window_docs = lax.dynamic_slice(padded, (position, 0), (SPAN, TOKENS)).reshape(WINDOW)
    own_docs = document_numbers.reshape(TOKENS)
    key_pos = jnp.arange(WINDOW, dtype=jnp.int32) - (SPAN - 1) * TOKENS
    visible = (window_docs[:, None] == own_docs[None, :]) & (
        key_pos[:, None] <= jnp.arange(TOKENS, dtype=jnp.int32)[None, :]
    )
    bias = jnp.where(visible, 0.0, -jnp.inf).astype(F32)

    probs, contrib = attention(queries, output_gradient, adapter_up_weight, key_pairs, bias)
    for distance in (4, 2, 1):
        lanes = distance * TOKENS
        sent = from_behind(contrib[:, :lanes].astype(BF16), -distance)
        contrib = contrib[:, lanes:] + sent.astype(F32)
    key_grad = contrib.astype(BF16)
    up_share = mixed_share(probs, rank_window, output_gradient)

    shares = plain(
        shares_kernel,
        "shares",
        jax.ShapeDtypeStruct((2, ADAPTER_RANK, LANES), BF16),
        key_grad,
        hidden,
        up_share,
    )
    shares = exchange(shares.reshape(N_DP, 8, LANES), "dp")
    shares = plain(
        fold_dp_kernel, "fold_dp", jax.ShapeDtypeStruct((N_FSDP, 8, 384), F32), shares
    )
    shares = exchange(shares, "fsdp")
    shares = plain(
        fold_fsdp_kernel, "fold_fsdp", jax.ShapeDtypeStruct((N_DP, 8, 384), F32), shares
    )
    shares = exchange(shares, "dp")
    down, up = plain(
        spread_kernel,
        "spread",
        (
            jax.ShapeDtypeStruct((ADAPTER_RANK, 256), F32),
            jax.ShapeDtypeStruct((ADAPTER_RANK, KEY_HEADS * HEAD_SIZE), F32),
        ),
        shares,
    )
    return (down.T, up)


def solution(mesh):
    in_specs = (
        P(("dp", "fsdp"), None),
        P(("dp", "fsdp"), None),
        P(("dp", "fsdp"), None),
        P("dp", "fsdp"),
        P("fsdp", None),
        P(),
        P(("dp", "fsdp"), None),
    )
    out_specs = (P("fsdp", None), P())
    return jax.shard_map(local, mesh=mesh, in_specs=in_specs, out_specs=out_specs, check_vma=False)
```

```python
import functools
import math

import jax
import jax.numpy as jnp
from jax import lax
from jax.experimental import pallas as pl
from jax.experimental.pallas import tpu as pltpu
from jax.sharding import PartitionSpec as P

QUERY_HEADS = 32
KEY_HEADS = 4
HEAD_SIZE = 128
ADAPTER_RANK = 64
SPAN = 8
TOKENS = 128
WINDOW = SPAN * TOKENS
N_DP = 16
N_FSDP = 32
MODEL_WIDTH = 8192
VMEM_LIMIT = 20 * 1024 * 1024
BF16 = jnp.bfloat16
F32 = jnp.float32
NT = (((1,), (1,)), ((), ()))


def whole(*arrays):
    return [pl.BlockSpec(memory_space=pltpu.VMEM) for _ in arrays]


def params():
    return pltpu.CompilerParams(vmem_limit_bytes=VMEM_LIMIT)


def from_behind(block, distance):
    route = [(i, i + distance) for i in range(N_FSDP) if 0 <= i + distance < N_FSDP]
    return lax.ppermute(block, "fsdp", route)


def exchange(slots, axis):
    return lax.all_to_all(slots, axis, 0, 0, tiled=True)


def lowrank_kernel(weight_ref, hidden_ref, out_ref):
    total = jnp.zeros((ADAPTER_RANK, TOKENS), F32)
    for f in range(N_FSDP):
        rows = jnp.concatenate(
            [weight_ref[half, :, f * 128 : f * 128 + 128] for half in range(2)], axis=1
        )
        total += lax.dot_general(
            rows, hidden_ref[:, f * 256 : f * 256 + 256], NT, preferred_element_type=F32
        )
    out_ref[...] = total.astype(BF16)


def score_kernel(query_ref, keys_ref, bias_ref, weights_ref, stats_ref):
    factor = math.log2(math.e) / math.sqrt(HEAD_SIZE)

    def key_head(g, carry):
        keys = keys_ref[:, pl.ds(pl.multiple_of(g * HEAD_SIZE, HEAD_SIZE), HEAD_SIZE)]
        for m in range(QUERY_HEADS // KEY_HEADS):
            lanes = pl.ds(pl.multiple_of((g * 8 + m) * 128, 128), 128)
            scores = lax.dot_general(keys, query_ref[:, lanes], NT, preferred_element_type=F32)
            scores = scores + bias_ref[...]
            top = jnp.maximum(jnp.max(scores, axis=0, keepdims=True), -1e30) * factor
            weights = jnp.exp2(scores * factor - top)
            stats_ref[0:1, lanes] = top
            stats_ref[1:2, lanes] = jnp.sum(weights, axis=0, keepdims=True)
            weights_ref[:, lanes] = weights.astype(BF16)
        return carry

    lax.fori_loop(0, KEY_HEADS, key_head, 0)


def score(queries, keys, bias):
    return plain(
        score_kernel,
        "score",
        (
            jax.ShapeDtypeStruct((2 * TOKENS, QUERY_HEADS * TOKENS), BF16),
            jax.ShapeDtypeStruct((2, QUERY_HEADS * TOKENS), F32),
        ),
        queries,
        keys,
        bias,
    )


def reached_kernel(gradient_ref, up_ref, out_ref):
    def key_head(g, carry):
        up = up_ref[:, pl.ds(pl.multiple_of(g * HEAD_SIZE, HEAD_SIZE), HEAD_SIZE)]
        for m in range(QUERY_HEADS // KEY_HEADS):
            lanes = pl.ds(pl.multiple_of((g * 8 + m) * 128, 128), 128)
            out_ref[:, lanes] = lax.dot_general(
                up, gradient_ref[:, lanes], NT, preferred_element_type=F32
            )
        return carry

    lax.fori_loop(0, KEY_HEADS, key_head, 0)


def sums_of(weights_ref, scale, reached):
    shares = (reached.astype(BF16).astype(F32) * scale).astype(BF16)
    return lax.dot_general(weights_ref[...], shares, NT, preferred_element_type=F32).T


def far_kernel(w3_ref, w2_ref, s3_ref, s2_ref, s1_ref, s0_ref, reached_ref, far_ref, scale_ref):
    stats = [ref[...] for ref in (s3_ref, s2_ref, s1_ref, s0_ref)]
    top = stats[0][0:1]
    for s in stats[1:]:
        top = jnp.maximum(top, s[0:1])
    parts = [jnp.exp2(s[0:1] - top) for s in stats]
    inverse = 1.0 / sum(part * s[1:2] for part, s in zip(parts, stats))
    scales = [part * inverse for part in parts]
    for i, scale in enumerate(scales):
        scale_ref[i : i + 1, :] = scale
    reached = reached_ref[...]
    far_ref[:, :256] = sums_of(w3_ref, scales[0], reached).astype(BF16)
    far_ref[:, 256:] = sums_of(w2_ref, scales[1], reached).astype(BF16)


def near_kernel(w1_ref, w0_ref, scale_ref, reached_ref, near_ref):
    reached = reached_ref[...]
    near_ref[:, :256] = sums_of(w1_ref, scale_ref[2:3, :], reached)
    near_ref[:, 256:] = sums_of(w0_ref, scale_ref[3:4, :], reached)


def mixed_kernel(first, w3_ref, w2_ref, w1_ref, w0_ref, scale_ref, rank_ref, gradient_ref, out_ref):
    for g in range(2):
        share = jnp.zeros((ADAPTER_RANK, HEAD_SIZE), F32)
        for m in range(QUERY_HEADS // KEY_HEADS):
            h = (first + g) * 8 + m
            lanes = slice(h * 128, h * 128 + 128)
            mixed = jnp.zeros((ADAPTER_RANK, TOKENS), F32)
            for i, ref in enumerate((w3_ref, w2_ref, w1_ref, w0_ref)):
                rank = rank_ref[:, i * 256 : i * 256 + 256]
                part = jnp.dot(rank, ref[:, lanes], preferred_element_type=F32)
                mixed += part * scale_ref[i : i + 1, lanes]
            share += jnp.dot(
                mixed.astype(BF16), gradient_ref[:, lanes], preferred_element_type=F32
            )
        out_ref[:, g * 128 : g * 128 + 128] = share


DOWN = N_FSDP * 128
LANES = DOWN + 256


def shares_kernel(key_ref, hidden_ref, up0_ref, up1_ref, out_ref):
    for f in range(N_FSDP):
        product = jnp.dot(
            key_ref[...], hidden_ref[:, f * 256 : f * 256 + 256], preferred_element_type=F32
        ).astype(BF16)
        for half in range(2):
            out_ref[half, :, f * 128 : f * 128 + 128] = product[:, half * 128 : half * 128 + 128]
    for half, up_ref in enumerate((up0_ref, up1_ref)):
        out_ref[half, :, DOWN:] = up_ref[...].astype(BF16)


def fold_dp_kernel(in_ref, out_ref):
    def total(columns):
        return sum(in_ref[d, :, columns].astype(F32) for d in range(N_DP))

    up = total(slice(DOWN, LANES)).astype(BF16)
    for f in range(N_FSDP):
        out_ref[f, :, :128] = total(slice(f * 128, f * 128 + 128)).astype(BF16)
        out_ref[f, :, 128:] = up


def fold_fsdp_kernel(in_ref, out_ref):
    total = sum(in_ref[f].astype(F32) for f in range(N_FSDP))
    for d in range(N_DP):
        out_ref[d] = total


def spread_kernel(in_ref, down_ref, up_ref):
    for half in range(2):
        for part in range(8):
            rows = slice(part * 8, part * 8 + 8)
            block = in_ref[half * 8 + part]
            down_ref[rows, half * 128 : half * 128 + 128] = block[:, :128]
            up_ref[rows, half * 256 : half * 256 + 256] = block[:, 128:]


def plain(kernel, name, out_shape, *arrays):
    return pl.pallas_call(
        kernel,
        in_specs=whole(*arrays),
        out_specs=jax.tree.map(lambda _: pl.BlockSpec(memory_space=pltpu.VMEM), out_shape),
        out_shape=out_shape,
        compiler_params=params(),
        cost_estimate=pl.CostEstimate(flops=10**10, bytes_accessed=2**27, transcendentals=0),
        name=name,
    )(*arrays)


def local(
    hidden, queries, keys, document_numbers, adapter_down_weight, adapter_up_weight, output_gradient
):
    position = lax.axis_index("fsdp")
    member = lax.axis_index("dp")
    half, part = member // 8, member % 8

    keys1, keys2, keys3 = [from_behind(keys, distance) for distance in (1, 2, 3)]
    weight_slice = lax.dynamic_slice(adapter_down_weight.T, (part * 8, half * 128), (8, 128))
    docs_row = document_numbers.reshape(1, TOKENS).astype(BF16)
    slot = jnp.concatenate([weight_slice, docs_row, jnp.zeros((7, 128), BF16)], axis=0)
    slots = jnp.broadcast_to(slot[None], (N_FSDP, 16, 128))
    row_parts = exchange(slots, "fsdp")
    pair0 = jnp.concatenate([keys1, keys], axis=0)
    pair1 = jnp.concatenate([keys3, keys2], axis=0)
    pair2 = from_behind(pair1, 2)
    weight_part = row_parts[:, :8].transpose(1, 0, 2).reshape(1, 8, DOWN)
    docs = row_parts[:, 8].astype(jnp.int32)
    weight_slots = jnp.broadcast_to(weight_part, (N_DP, 8, DOWN))
    weight = exchange(weight_slots, "dp").reshape(2, ADAPTER_RANK, DOWN)
    pair2 = lax.optimization_barrier((pair2, weight_slots))[0]
    pair3 = from_behind(pair2, 2)

    padded = jnp.concatenate([jnp.full((SPAN - 1, TOKENS), -1, jnp.int32), docs], axis=0)
    window_docs = lax.dynamic_slice(padded, (position, 0), (SPAN, TOKENS)).reshape(WINDOW)
    own_docs = document_numbers.reshape(TOKENS)
    key_pos = jnp.arange(WINDOW, dtype=jnp.int32) - (SPAN - 1) * TOKENS
    visible = (window_docs[:, None] == own_docs[None, :]) & (
        key_pos[:, None] <= jnp.arange(TOKENS, dtype=jnp.int32)[None, :]
    )
    bias = jnp.where(visible, 0.0, -jnp.inf).astype(F32)
    biases = [bias[i * 256 : i * 256 + 256] for i in range(4)]

    reached = plain(
        reached_kernel,
        "reached",
        jax.ShapeDtypeStruct((ADAPTER_RANK, QUERY_HEADS * TOKENS), F32),
        output_gradient,
        adapter_up_weight,
    )
    w0, s0 = score(queries, pair0, biases[3])
    w1, s1 = score(queries, pair1, biases[2])
    pair2, w1 = lax.optimization_barrier((pair2, w1))
    w2, s2 = score(queries, pair2, biases[1])
    rank = plain(
        lowrank_kernel, "lowrank", jax.ShapeDtypeStruct((ADAPTER_RANK, TOKENS), BF16), weight, hidden
    )
    rank1 = jnp.concatenate([from_behind(rank, 1), rank], axis=1)
    pair3, w2, rank = lax.optimization_barrier((pair3, w2, rank))
    w3, s3 = score(queries, pair3, biases[0])
    w3, rank1 = lax.optimization_barrier((w3, rank1))
    rank2 = jnp.concatenate([from_behind(rank1, 2), rank1], axis=1)
    far, scale = plain(
        far_kernel,
        "far",
        (
            jax.ShapeDtypeStruct((ADAPTER_RANK, WINDOW // 2), BF16),
            jax.ShapeDtypeStruct((4, QUERY_HEADS * TOKENS), F32),
        ),
        w3,
        w2,
        s3,
        s2,
        s1,
        s0,
        reached,
    )
    near = plain(
        near_kernel,
        "near",
        jax.ShapeDtypeStruct((ADAPTER_RANK, WINDOW // 2), F32),
        w1,
        w0,
        scale,
        reached,
    )
    came = from_behind(far, -4)
    came, rank2 = lax.optimization_barrier((came, rank2))
    near = near + came.astype(F32)
    rank3 = jnp.concatenate([from_behind(rank2, 4), rank2], axis=1)
    came = from_behind(near[:, :256], -2)
    came, rank3 = lax.optimization_barrier((came, rank3))
    near = near[:, 256:] + came
    came = from_behind(near[:, :128], -1)
    ups = [
        plain(
            functools.partial(mixed_kernel, first),
            "mixed",
            jax.ShapeDtypeStruct((ADAPTER_RANK, 2 * HEAD_SIZE), F32),
            w3,
            w2,
            w1,
            w0,
            scale,
            rank3,
            output_gradient,
        )
        for first in (0, 2)
    ]
    key_grad = (near[:, 128:] + came).astype(BF16)

    shares = plain(
        shares_kernel,
        "shares",
        jax.ShapeDtypeStruct((2, ADAPTER_RANK, LANES), BF16),
        key_grad,
        hidden,
        *ups,
    )
    shares = exchange(shares.reshape(N_DP, 8, LANES), "dp")
    shares = plain(
        fold_dp_kernel, "fold_dp", jax.ShapeDtypeStruct((N_FSDP, 8, 384), BF16), shares
    )
    shares = exchange(shares, "fsdp")
    shares = plain(
        fold_fsdp_kernel, "fold_fsdp", jax.ShapeDtypeStruct((N_DP, 8, 384), F32), shares
    )
    shares = exchange(shares, "dp")
    down, up = plain(
        spread_kernel,
        "spread",
        (
            jax.ShapeDtypeStruct((ADAPTER_RANK, 256), F32),
            jax.ShapeDtypeStruct((ADAPTER_RANK, KEY_HEADS * HEAD_SIZE), F32),
        ),
        shares,
    )
    return (down.T, up)


def solution(mesh):
    in_specs = (
        P(("dp", "fsdp"), None),
        P(("dp", "fsdp"), None),
        P(("dp", "fsdp"), None),
        P("dp", "fsdp"),
        P("fsdp", None),
        P(),
        P(("dp", "fsdp"), None),
    )
    out_specs = (P("fsdp", None), P())
    return jax.shard_map(local, mesh=mesh, in_specs=in_specs, out_specs=out_specs, check_vma=False)
```

```python
import math

import jax
import jax.numpy as jnp
from jax import lax
from jax.experimental import pallas as pl
from jax.experimental.pallas import tpu as pltpu
from jax.sharding import PartitionSpec as P

QUERY_HEADS = 32
KEY_HEADS = 4
HEAD_SIZE = 128
ADAPTER_RANK = 64
SPAN = 8
TOKENS = 128
WINDOW = SPAN * TOKENS
N_DP = 16
N_FSDP = 32
MODEL_WIDTH = 8192
VMEM_LIMIT = 60 * 1024 * 1024
GROUP = QUERY_HEADS // KEY_HEADS
COST = pl.CostEstimate(flops=10**10, bytes_accessed=2**27, transcendentals=0)
BF16 = jnp.bfloat16
F32 = jnp.float32
NT = (((1,), (1,)), ((), ()))


def whole(*arrays):
    return [pl.BlockSpec(memory_space=pltpu.VMEM) for _ in arrays]


def params():
    return pltpu.CompilerParams(vmem_limit_bytes=VMEM_LIMIT)


def from_behind(block, distance):
    route = [(i, i + distance) for i in range(N_FSDP) if 0 <= i + distance < N_FSDP]
    return lax.ppermute(block, "fsdp", route)


def exchange(slots, axis):
    return lax.all_to_all(slots, axis, 0, 0, tiled=True)


def lowrank_kernel(weight_ref, hidden_ref, out_ref, total_ref):
    step = pl.program_id(0)
    total = jnp.zeros((ADAPTER_RANK, TOKENS), F32)
    for f in range(8):
        rows = jnp.concatenate(
            [weight_ref[half, :, f * 128 : f * 128 + 128] for half in range(2)], axis=1
        )
        total += lax.dot_general(
            rows, hidden_ref[:, f * 256 : f * 256 + 256], NT, preferred_element_type=F32
        )

    @pl.when(step == 0)
    def _():
        total_ref[...] = total

    @pl.when(step > 0)
    def _():
        total_ref[...] += total

    @pl.when(step == 3)
    def _():
        out_ref[...] = total_ref[...].astype(BF16)


def score_pair(query_ref, keys, bias_ref, rows, weights_ref, stats_ref, at):
    factor = math.log2(math.e) / math.sqrt(HEAD_SIZE)
    for m in range(GROUP):
        lanes = slice(m * 128, m * 128 + 128)
        scores = lax.dot_general(keys, query_ref[:, lanes], NT, preferred_element_type=F32)
        scores = scores + bias_ref[rows, :]
        top = jnp.maximum(jnp.max(scores, axis=0, keepdims=True), -1e30) * factor
        weights = jnp.exp2(scores * factor - top)
        stats_ref[at : at + 1, lanes] = top
        stats_ref[at + 1 : at + 2, lanes] = jnp.sum(weights, axis=0, keepdims=True)
        weights_ref[:, lanes] = weights.astype(BF16)


def score_kernel(
    query_ref,
    keys2_ref,
    keys1_ref,
    keys0_ref,
    bias_ref,
    w2_ref,
    w1_ref,
    w0_ref,
    stats_ref,
):
    refs = ((keys2_ref, w2_ref), (keys1_ref, w1_ref), (keys0_ref, w0_ref))
    for i, (keys_ref, w_ref) in enumerate(refs):
        rows = slice(256 + i * 256, 512 + i * 256)
        score_pair(query_ref, keys_ref[...], bias_ref, rows, w_ref, stats_ref, 2 * i)
    stats_ref[6:8, :] = jnp.zeros((2, GROUP * TOKENS), F32)


def reached_kernel(gradient_ref, up_ref, reached_ref):
    for m in range(GROUP):
        lanes = slice(m * 128, m * 128 + 128)
        reached_ref[:, lanes] = lax.dot_general(
            up_ref[...], gradient_ref[:, lanes], NT, preferred_element_type=F32
        ).astype(BF16)


def sums_of(weights_ref, scale, reached):
    shares = (reached * scale).astype(BF16)
    return lax.dot_general(weights_ref[...], shares, NT, preferred_element_type=F32)


def add_up(sums_ref, out_ref, pairs):
    step = pl.program_id(0)
    for i, sums in enumerate(pairs):
        rows = slice(i * 256, i * 256 + 256)

        @pl.when(step == 0)
        def _(rows=rows, sums=sums):
            sums_ref[rows, :] = sums

        @pl.when(step > 0)
        def _(rows=rows, sums=sums):
            sums_ref[rows, :] += sums

    @pl.when(step == KEY_HEADS - 1)
    def _():
        out_ref[...] = sums_ref[...].T.astype(out_ref.dtype)


def far_kernel(
    query_ref,
    keys3_ref,
    bias_ref,
    w2_ref,
    stats_ref,
    reached_ref,
    w3_ref,
    scale_ref,
    far_ref,
    own_ref,
    sums_ref,
):
    score_pair(query_ref, keys3_ref[...], bias_ref, slice(0, 256), w3_ref, own_ref, 0)
    stats = [own_ref[0:2, :]] + [stats_ref[2 * i : 2 * i + 2, :] for i in range(3)]
    top = stats[0][0:1]
    for s in stats[1:]:
        top = jnp.maximum(top, s[0:1])
    parts = [jnp.exp2(s[0:1] - top) for s in stats]
    inverse = 1.0 / sum(part * s[1:2] for part, s in zip(parts, stats))
    scales = [part * inverse for part in parts]
    for i, scale in enumerate(scales):
        scale_ref[i : i + 1, :] = scale
    reached = reached_ref[...].astype(F32)
    pairs = [sums_of(w3_ref, scales[0], reached), sums_of(w2_ref, scales[1], reached)]
    add_up(sums_ref, far_ref, pairs)


def near_kernel(w1_ref, w0_ref, scale_ref, reached_ref, near_ref, sums_ref):
    reached = reached_ref[...].astype(F32)
    pairs = [
        sums_of(w1_ref, scale_ref[2:3, :], reached),
        sums_of(w0_ref, scale_ref[3:4, :], reached),
    ]
    add_up(sums_ref, near_ref, pairs)


def mixed_kernel(w3_ref, w2_ref, w1_ref, w0_ref, scale_ref, rank_ref, gradient_ref, out_ref):
    share = jnp.zeros((ADAPTER_RANK, HEAD_SIZE), F32)
    for m in range(GROUP):
        lanes = slice(m * 128, m * 128 + 128)
        mixed = jnp.zeros((ADAPTER_RANK, TOKENS), F32)
        for i, ref in enumerate((w3_ref, w2_ref, w1_ref, w0_ref)):
            rank = rank_ref[:, i * 256 : i * 256 + 256]
            part = jnp.dot(rank, ref[:, lanes], preferred_element_type=F32)
            mixed += part * scale_ref[i : i + 1, lanes]
        share += jnp.dot(mixed.astype(BF16), gradient_ref[:, lanes], preferred_element_type=F32)
    out_ref[...] = share


DOWN = N_FSDP * 128
LANES = DOWN + 256


def shares_kernel(key_ref, hidden_ref, up0_ref, up1_ref, out_ref):
    step = pl.program_id(0)
    for f in range(8):
        product = jnp.dot(
            key_ref[...], hidden_ref[:, f * 256 : f * 256 + 256], preferred_element_type=F32
        ).astype(BF16)
        lanes = pl.ds(pl.multiple_of(step * 1024 + f * 128, 128), 128)
        for half in range(2):
            out_ref[half, :, lanes] = product[:, half * 128 : half * 128 + 128]

    @pl.when(step == 0)
    def _():
        for half, up_ref in enumerate((up0_ref, up1_ref)):
            out_ref[half, :, DOWN:] = up_ref[...].astype(BF16)


def fold_dp_kernel(in_ref, out_ref):
    def total(columns):
        return sum(in_ref[d, :, columns].astype(F32) for d in range(N_DP))

    up = total(slice(DOWN, LANES)).astype(BF16)
    for f in range(N_FSDP):
        out_ref[f, :, :128] = total(slice(f * 128, f * 128 + 128)).astype(BF16)
        out_ref[f, :, 128:] = up


def fold_fsdp_kernel(in_ref, out_ref):
    total = sum(in_ref[f].astype(F32) for f in range(N_FSDP))
    for d in range(N_DP):
        out_ref[d] = total


def spread_kernel(in_ref, down_ref, up_ref):
    for half in range(2):
        for part in range(8):
            rows = slice(part * 8, part * 8 + 8)
            block = in_ref[half * 8 + part]
            down_ref[rows, half * 128 : half * 128 + 128] = block[:, :128]
            up_ref[rows, half * 256 : half * 256 + 256] = block[:, 128:]


def plain(kernel, name, out_shape, *arrays):
    return pl.pallas_call(
        kernel,
        in_specs=whole(*arrays),
        out_specs=jax.tree.map(lambda _: pl.BlockSpec(memory_space=pltpu.VMEM), out_shape),
        out_shape=out_shape,
        compiler_params=params(),
        cost_estimate=COST,
        name=name,
    )(*arrays)


def by_steps(kernel, name, steps, out_specs, out_shape, given, scratch=()):
    return pl.pallas_call(
        kernel,
        grid=(steps,),
        in_specs=[spec for spec, _ in given],
        out_specs=out_specs,
        out_shape=out_shape,
        scratch_shapes=list(scratch),
        compiler_params=params(),
        cost_estimate=COST,
        name=name,
    )(*[array for _, array in given])


def columns(rows, lanes, first=0):
    return pl.BlockSpec((rows, lanes), lambda g: (0, first + g))


def fixed(*shape):
    return pl.BlockSpec(shape, lambda g: (0,) * len(shape))


def local(
    hidden, queries, keys, document_numbers, adapter_down_weight, adapter_up_weight, output_gradient
):
    position = lax.axis_index("fsdp")
    member = lax.axis_index("dp")
    half, part = member // 8, member % 8

    keys1, keys2, keys3 = [from_behind(keys, distance) for distance in (1, 2, 3)]
    weight_slice = lax.dynamic_slice(adapter_down_weight.T, (part * 8, half * 128), (8, 128))
    docs_row = document_numbers.reshape(1, TOKENS).astype(BF16)
    slot = jnp.concatenate([weight_slice, docs_row, jnp.zeros((7, 128), BF16)], axis=0)
    slots = jnp.broadcast_to(slot[None], (N_FSDP, 16, 128))
    row_parts = exchange(slots, "fsdp")
    pair0 = jnp.concatenate([keys1, keys], axis=0)
    pair1 = jnp.concatenate([keys3, keys2], axis=0)
    pair2 = from_behind(pair1, 2)
    weight_part = row_parts[:, :8].transpose(1, 0, 2).reshape(1, 8, DOWN)
    docs = row_parts[:, 8].astype(jnp.int32)
    weight_slots = jnp.broadcast_to(weight_part, (N_DP, 8, DOWN))
    weight = exchange(weight_slots, "dp").reshape(2, ADAPTER_RANK, DOWN)
    pair2 = lax.optimization_barrier((pair2, weight_slots))[0]
    pair3 = from_behind(pair2, 2)

    padded = jnp.concatenate([jnp.full((SPAN - 1, TOKENS), -1, jnp.int32), docs], axis=0)
    window_docs = lax.dynamic_slice(padded, (position, 0), (SPAN, TOKENS)).reshape(WINDOW)
    own_docs = document_numbers.reshape(TOKENS)
    key_pos = jnp.arange(WINDOW, dtype=jnp.int32) - (SPAN - 1) * TOKENS
    visible = (window_docs[:, None] == own_docs[None, :]) & (
        key_pos[:, None] <= jnp.arange(TOKENS, dtype=jnp.int32)[None, :]
    )
    bias = jnp.where(visible, 0.0, -jnp.inf).astype(F32)
    lanes = GROUP * TOKENS
    queries_by, keys_by, weights_by = columns(TOKENS, lanes), columns(256, 128), columns(256, lanes)
    weights_shape = jax.ShapeDtypeStruct((2 * TOKENS, QUERY_HEADS * TOKENS), BF16)
    stats_by, stats_shape = columns(8, lanes), jax.ShapeDtypeStruct((8, QUERY_HEADS * TOKENS), F32)
    reached_by = columns(ADAPTER_RANK, lanes)
    sums = pltpu.VMEM((512, ADAPTER_RANK), F32)
    reached = by_steps(
        reached_kernel,
        "reached",
        KEY_HEADS,
        reached_by,
        jax.ShapeDtypeStruct((ADAPTER_RANK, QUERY_HEADS * TOKENS), BF16),
        [
            (queries_by, output_gradient),
            (columns(ADAPTER_RANK, HEAD_SIZE), adapter_up_weight),
        ],
    )
    w2, w1, w0, stats = by_steps(
        score_kernel,
        "score",
        KEY_HEADS,
        [weights_by] * 3 + [stats_by],
        [weights_shape] * 3 + [stats_shape],
        [
            (queries_by, queries),
            (keys_by, pair2),
            (keys_by, pair1),
            (keys_by, pair0),
            (fixed(WINDOW, TOKENS), bias),
        ],
    )
    rank = by_steps(
        lowrank_kernel,
        "lowrank",
        4,
        fixed(ADAPTER_RANK, TOKENS),
        jax.ShapeDtypeStruct((ADAPTER_RANK, TOKENS), BF16),
        [
            (pl.BlockSpec((2, ADAPTER_RANK, 1024), lambda j: (0, 0, j)), weight),
            (columns(TOKENS, 2048), hidden),
        ],
        [pltpu.VMEM((ADAPTER_RANK, TOKENS), F32)],
    )
    rank1 = jnp.concatenate([from_behind(rank, 1), rank], axis=1)
    pair3, rank, stats = lax.optimization_barrier((pair3, rank, stats))
    w3, scale, far = by_steps(
        far_kernel,
        "far",
        KEY_HEADS,
        [weights_by, stats_by, fixed(ADAPTER_RANK, WINDOW // 2)],
        [weights_shape, stats_shape, jax.ShapeDtypeStruct((ADAPTER_RANK, WINDOW // 2), BF16)],
        [
            (queries_by, queries),
            (keys_by, pair3),
            (fixed(256, TOKENS), bias),
            (weights_by, w2),
            (stats_by, stats),
            (reached_by, reached),
        ],
        [pltpu.VMEM((8, lanes), F32), sums],
    )
    near = by_steps(
        near_kernel,
        "near",
        KEY_HEADS,
        fixed(ADAPTER_RANK, WINDOW // 2),
        jax.ShapeDtypeStruct((ADAPTER_RANK, WINDOW // 2), F32),
        [(weights_by, w1), (weights_by, w0), (stats_by, scale), (reached_by, reached)],
        [sums],
    )
    came = from_behind(far, -4)
    rank2 = jnp.concatenate([from_behind(rank1, 2), rank1], axis=1)
    near = near + came.astype(F32)
    rank3 = jnp.concatenate([from_behind(rank2, 4), rank2], axis=1)
    came = from_behind(near[:, :256], -2)
    near = near[:, 256:] + came
    came = from_behind(near[:, :128], -1)
    ups = [
        by_steps(
            mixed_kernel,
            "mixed",
            2,
            columns(ADAPTER_RANK, HEAD_SIZE),
            jax.ShapeDtypeStruct((ADAPTER_RANK, 2 * HEAD_SIZE), F32),
            [(columns(256, lanes, first), w) for w in (w3, w2, w1, w0)]
            + [
                (columns(8, lanes, first), scale),
                (fixed(ADAPTER_RANK, WINDOW), rank3),
                (columns(TOKENS, lanes, first), output_gradient),
            ],
        )
        for first in (0, 2)
    ]
    key_grad = (near[:, 128:] + came).astype(BF16)

    shares = by_steps(
        shares_kernel,
        "shares",
        4,
        fixed(2, ADAPTER_RANK, LANES),
        jax.ShapeDtypeStruct((2, ADAPTER_RANK, LANES), BF16),
        [
            (fixed(ADAPTER_RANK, TOKENS), key_grad),
            (columns(TOKENS, 2048), hidden),
            (fixed(ADAPTER_RANK, 256), ups[0]),
            (fixed(ADAPTER_RANK, 256), ups[1]),
        ],
    )
    shares = exchange(shares.reshape(N_DP, 8, LANES), "dp")
    shares = plain(
        fold_dp_kernel, "fold_dp", jax.ShapeDtypeStruct((N_FSDP, 8, 384), BF16), shares
    )
    shares = exchange(shares, "fsdp")
    shares = plain(
        fold_fsdp_kernel, "fold_fsdp", jax.ShapeDtypeStruct((N_DP, 8, 384), F32), shares
    )
    shares = exchange(shares, "dp")
    down, up = plain(
        spread_kernel,
        "spread",
        (
            jax.ShapeDtypeStruct((ADAPTER_RANK, 256), F32),
            jax.ShapeDtypeStruct((ADAPTER_RANK, KEY_HEADS * HEAD_SIZE), F32),
        ),
        shares,
    )
    return (down.T, up)


def solution(mesh):
    in_specs = (
        P(("dp", "fsdp"), None),
        P(("dp", "fsdp"), None),
        P(("dp", "fsdp"), None),
        P("dp", "fsdp"),
        P("fsdp", None),
        P(),
        P(("dp", "fsdp"), None),
    )
    out_specs = (P("fsdp", None), P())
    return jax.shard_map(local, mesh=mesh, in_specs=in_specs, out_specs=out_specs, check_vma=False)
```

```python
import functools
import math

import jax
import jax.numpy as jnp
from jax import lax
from jax.experimental import pallas as pl
from jax.experimental.pallas import tpu as pltpu
from jax.sharding import PartitionSpec as P

QUERY_HEADS = 32
KEY_HEADS = 4
HEAD_SIZE = 128
ADAPTER_RANK = 64
SPAN = 8
TOKENS = 128
WINDOW = SPAN * TOKENS
N_DP = 16
N_FSDP = 32
MODEL_WIDTH = 8192
GROUP = QUERY_HEADS // KEY_HEADS
COST = pl.CostEstimate(flops=10**10, bytes_accessed=2**27, transcendentals=0)
BF16 = jnp.bfloat16
F32 = jnp.float32
NT = (((1,), (1,)), ((), ()))


def whole(*arrays):
    return [pl.BlockSpec(memory_space=pltpu.VMEM) for _ in arrays]


def params(mebibytes):
    return pltpu.CompilerParams(vmem_limit_bytes=mebibytes * 1024 * 1024)


def from_behind(block, distance):
    route = [(i, i + distance) for i in range(N_FSDP) if 0 <= i + distance < N_FSDP]
    return lax.ppermute(block, "fsdp", route)


def exchange(slots, axis):
    return lax.all_to_all(slots, axis, 0, 0, tiled=True)


def lowrank_kernel(weight_hbm, hidden_hbm, out_ref, weight_ref, hidden_ref, arrived):
    copies = []
    for j in range(4):
        lanes = pl.ds(j * 1024, 1024)
        wide = pl.ds(j * 2048, 2048)
        copies.append(
            (
                pltpu.make_async_copy(
                    weight_hbm.at[:, :, lanes], weight_ref.at[:, :, lanes], arrived.at[0, j]
                ),
                pltpu.make_async_copy(
                    hidden_hbm.at[:, wide], hidden_ref.at[:, wide], arrived.at[1, j]
                ),
            )
        )
    for pair in copies:
        for copy in pair:
            copy.start()
    total = jnp.zeros((ADAPTER_RANK, TOKENS), F32)
    for j, pair in enumerate(copies):
        for copy in pair:
            copy.wait()
        for f in range(8 * j, 8 * j + 8):
            rows = jnp.concatenate(
                [weight_ref[half, :, f * 128 : f * 128 + 128] for half in range(2)], axis=1
            )
            total += lax.dot_general(
                rows, hidden_ref[:, f * 256 : f * 256 + 256], NT, preferred_element_type=F32
            )
    out_ref[...] = total.astype(BF16)


def score_pair(query_ref, keys, bias_ref, rows, weights_ref, stats_ref, at):
    factor = math.log2(math.e) / math.sqrt(HEAD_SIZE)
    for m in range(GROUP):
        lanes = slice(m * 128, m * 128 + 128)
        scores = lax.dot_general(keys, query_ref[:, lanes], NT, preferred_element_type=F32)
        scores = scores + bias_ref[rows, :]
        top = jnp.maximum(jnp.max(scores, axis=0, keepdims=True), -1e30) * factor
        weights = jnp.exp2(scores * factor - top)
        stats_ref[at : at + 1, lanes] = top
        stats_ref[at + 1 : at + 2, lanes] = jnp.sum(weights, axis=0, keepdims=True)
        weights_ref[:, lanes] = weights.astype(BF16)


def score_kernel(
    query_ref,
    keys2_ref,
    keys1_ref,
    keys0_ref,
    bias_ref,
    w2_ref,
    w1_ref,
    w0_ref,
    stats_ref,
):
    refs = ((keys2_ref, w2_ref), (keys1_ref, w1_ref), (keys0_ref, w0_ref))
    for i, (keys_ref, w_ref) in enumerate(refs):
        rows = slice(256 + i * 256, 512 + i * 256)
        score_pair(query_ref, keys_ref[...], bias_ref, rows, w_ref, stats_ref, 2 * i)
    stats_ref[6:8, :] = jnp.zeros((2, GROUP * TOKENS), F32)


def last_score_kernel(query_ref, keys_ref, bias_ref, weights_ref, stats_ref):
    def key_head(g, carry):
        keys = keys_ref[:, pl.ds(pl.multiple_of(g * HEAD_SIZE, HEAD_SIZE), HEAD_SIZE)]
        lanes = pl.ds(pl.multiple_of(g * GROUP * 128, 128), GROUP * 128)
        score_pair(
            query_ref.at[:, lanes],
            keys,
            bias_ref,
            slice(0, 256),
            weights_ref.at[:, lanes],
            stats_ref.at[:, lanes],
            0,
        )
        return carry

    lax.fori_loop(0, KEY_HEADS, key_head, 0)


def reached_kernel(gradient_ref, up_ref, out_ref):
    def key_head(g, carry):
        up = up_ref[:, pl.ds(pl.multiple_of(g * HEAD_SIZE, HEAD_SIZE), HEAD_SIZE)]
        for m in range(GROUP):
            lanes = pl.ds(pl.multiple_of((g * GROUP + m) * 128, 128), 128)
            out_ref[:, lanes] = lax.dot_general(
                up, gradient_ref[:, lanes], NT, preferred_element_type=F32
            ).astype(BF16)
        return carry

    lax.fori_loop(0, KEY_HEADS, key_head, 0)


def sums_of(weights_ref, scale, reached):
    shares = (reached * scale).astype(BF16)
    return lax.dot_general(weights_ref[...], shares, NT, preferred_element_type=F32).T


def far_kernel(w3_ref, w2_ref, last_ref, stats_ref, reached_ref, far_ref, scale_ref):
    stats = [last_ref[...]] + [stats_ref[2 * i : 2 * i + 2, :] for i in range(3)]
    top = stats[0][0:1]
    for s in stats[1:]:
        top = jnp.maximum(top, s[0:1])
    parts = [jnp.exp2(s[0:1] - top) for s in stats]
    inverse = 1.0 / sum(part * s[1:2] for part, s in zip(parts, stats))
    scales = [part * inverse for part in parts]
    for i, scale in enumerate(scales):
        scale_ref[i : i + 1, :] = scale
    reached = reached_ref[...].astype(F32)
    far_ref[:, :256] = sums_of(w3_ref, scales[0], reached).astype(BF16)
    far_ref[:, 256:] = sums_of(w2_ref, scales[1], reached).astype(BF16)


def near_kernel(w1_ref, w0_ref, scale_ref, reached_ref, near_ref):
    reached = reached_ref[...].astype(F32)
    near_ref[:, :256] = sums_of(w1_ref, scale_ref[2:3, :], reached)
    near_ref[:, 256:] = sums_of(w0_ref, scale_ref[3:4, :], reached)


def mixed_kernel(first, w3_ref, w2_ref, w1_ref, w0_ref, scale_ref, rank_ref, gradient_ref, out_ref):
    for g in range(2):
        share = jnp.zeros((ADAPTER_RANK, HEAD_SIZE), F32)
        for m in range(QUERY_HEADS // KEY_HEADS):
            h = (first + g) * 8 + m
            lanes = slice(h * 128, h * 128 + 128)
            mixed = jnp.zeros((ADAPTER_RANK, TOKENS), F32)
            for i, ref in enumerate((w3_ref, w2_ref, w1_ref, w0_ref)):
                rank = rank_ref[:, i * 256 : i * 256 + 256]
                part = jnp.dot(rank, ref[:, lanes], preferred_element_type=F32)
                mixed += part * scale_ref[i : i + 1, lanes]
            share += jnp.dot(
                mixed.astype(BF16), gradient_ref[:, lanes], preferred_element_type=F32
            )
        out_ref[:, g * 128 : g * 128 + 128] = share


DOWN = N_FSDP * 128
LANES = DOWN + 256


def shares_kernel(key_ref, hidden_ref, up0_ref, up1_ref, out_ref):
    for f in range(N_FSDP):
        product = jnp.dot(
            key_ref[...], hidden_ref[:, f * 256 : f * 256 + 256], preferred_element_type=F32
        ).astype(BF16)
        for half in range(2):
            out_ref[half, :, f * 128 : f * 128 + 128] = product[:, half * 128 : half * 128 + 128]
    for half, up_ref in enumerate((up0_ref, up1_ref)):
        out_ref[half, :, DOWN:] = up_ref[...].astype(BF16)


def fold_dp_kernel(in_ref, out_ref):
    def total(columns):
        return sum(in_ref[d, :, columns].astype(F32) for d in range(N_DP))

    up = total(slice(DOWN, LANES)).astype(BF16)
    for f in range(N_FSDP):
        out_ref[f, :, :128] = total(slice(f * 128, f * 128 + 128)).astype(BF16)
        out_ref[f, :, 128:] = up


def fold_fsdp_kernel(in_ref, out_ref):
    total = sum(in_ref[f].astype(F32) for f in range(N_FSDP))
    for d in range(N_DP):
        out_ref[d] = total


def spread_kernel(in_ref, down_ref, up_ref):
    for half in range(2):
        for part in range(8):
            rows = slice(part * 8, part * 8 + 8)
            block = in_ref[half * 8 + part]
            down_ref[rows, half * 128 : half * 128 + 128] = block[:, :128]
            up_ref[rows, half * 256 : half * 256 + 256] = block[:, 128:]


def plain(kernel, name, out_shape, *arrays):
    return pl.pallas_call(
        kernel,
        in_specs=whole(*arrays),
        out_specs=jax.tree.map(lambda _: pl.BlockSpec(memory_space=pltpu.VMEM), out_shape),
        out_shape=out_shape,
        compiler_params=params(20),
        cost_estimate=COST,
        name=name,
    )(*arrays)


def by_steps(kernel, name, steps, out_specs, out_shape, given, scratch=()):
    return pl.pallas_call(
        kernel,
        grid=(steps,),
        in_specs=[spec for spec, _ in given],
        out_specs=out_specs,
        out_shape=out_shape,
        scratch_shapes=list(scratch),
        compiler_params=params(60),
        cost_estimate=COST,
        name=name,
    )(*[array for _, array in given])


def columns(rows, lanes, first=0):
    return pl.BlockSpec((rows, lanes), lambda g: (0, first + g))


def fixed(*shape):
    return pl.BlockSpec(shape, lambda g: (0,) * len(shape))


def local(
    hidden, queries, keys, document_numbers, adapter_down_weight, adapter_up_weight, output_gradient
):
    position = lax.axis_index("fsdp")
    member = lax.axis_index("dp")
    half, part = member // 8, member % 8

    keys1, keys2, keys3 = [from_behind(keys, distance) for distance in (1, 2, 3)]
    weight_slice = lax.dynamic_slice(adapter_down_weight.T, (part * 8, half * 128), (8, 128))
    docs_row = document_numbers.reshape(1, TOKENS).astype(BF16)
    slot = jnp.concatenate([weight_slice, docs_row, jnp.zeros((7, 128), BF16)], axis=0)
    slots = jnp.broadcast_to(slot[None], (N_FSDP, 16, 128))
    row_parts = exchange(slots, "fsdp")
    pair0 = jnp.concatenate([keys1, keys], axis=0)
    pair1 = jnp.concatenate([keys3, keys2], axis=0)
    pair2 = from_behind(pair1, 2)
    weight_part = row_parts[:, :8].transpose(1, 0, 2).reshape(1, 8, DOWN)
    docs = row_parts[:, 8].astype(jnp.int32)
    weight_slots = jnp.broadcast_to(weight_part, (N_DP, 8, DOWN))
    weight = exchange(weight_slots, "dp").reshape(2, ADAPTER_RANK, DOWN)
    pair2 = lax.optimization_barrier((pair2, weight_slots))[0]
    pair3 = from_behind(pair2, 2)

    padded = jnp.concatenate([jnp.full((SPAN - 1, TOKENS), -1, jnp.int32), docs], axis=0)
    window_docs = lax.dynamic_slice(padded, (position, 0), (SPAN, TOKENS)).reshape(WINDOW)
    own_docs = document_numbers.reshape(TOKENS)
    key_pos = jnp.arange(WINDOW, dtype=jnp.int32) - (SPAN - 1) * TOKENS
    visible = (window_docs[:, None] == own_docs[None, :]) & (
        key_pos[:, None] <= jnp.arange(TOKENS, dtype=jnp.int32)[None, :]
    )
    bias = jnp.where(visible, 0.0, -jnp.inf).astype(F32)
    lanes = GROUP * TOKENS
    columns_of = QUERY_HEADS * TOKENS
    queries_by, keys_by, weights_by = columns(TOKENS, lanes), columns(256, 128), columns(256, lanes)
    weights_shape = jax.ShapeDtypeStruct((2 * TOKENS, columns_of), BF16)
    w2, w1, w0, stats = by_steps(
        score_kernel,
        "score",
        KEY_HEADS,
        [weights_by] * 3 + [columns(8, lanes)],
        [weights_shape] * 3 + [jax.ShapeDtypeStruct((8, columns_of), F32)],
        [
            (queries_by, queries),
            (keys_by, pair2),
            (keys_by, pair1),
            (keys_by, pair0),
            (fixed(WINDOW, TOKENS), bias),
        ],
    )
    reached = plain(
        reached_kernel,
        "reached",
        jax.ShapeDtypeStruct((ADAPTER_RANK, columns_of), BF16),
        output_gradient,
        adapter_up_weight,
    )
    anywhere = pl.BlockSpec(memory_space=pl.ANY)
    rank = pl.pallas_call(
        lowrank_kernel,
        in_specs=[anywhere, anywhere],
        out_specs=pl.BlockSpec(memory_space=pltpu.VMEM),
        out_shape=jax.ShapeDtypeStruct((ADAPTER_RANK, TOKENS), BF16),
        scratch_shapes=[
            pltpu.VMEM((2, ADAPTER_RANK, DOWN), BF16),
            pltpu.VMEM((TOKENS, MODEL_WIDTH), BF16),
            pltpu.SemaphoreType.DMA((2, 4)),
        ],
        compiler_params=params(60),
        cost_estimate=COST,
        name="lowrank",
    )(weight, hidden)
    rank1 = jnp.concatenate([from_behind(rank, 1), rank], axis=1)
    pair3, rank, stats = lax.optimization_barrier((pair3, rank, stats))
    w3, last = plain(
        last_score_kernel,
        "last_score",
        (weights_shape, jax.ShapeDtypeStruct((2, columns_of), F32)),
        queries,
        pair3,
        bias[:256],
    )
    far, scale = plain(
        far_kernel,
        "far",
        (
            jax.ShapeDtypeStruct((ADAPTER_RANK, WINDOW // 2), BF16),
            jax.ShapeDtypeStruct((4, columns_of), F32),
        ),
        w3,
        w2,
        last,
        stats,
        reached,
    )
    near = plain(
        near_kernel,
        "near",
        jax.ShapeDtypeStruct((ADAPTER_RANK, WINDOW // 2), F32),
        w1,
        w0,
        scale,
        reached,
    )
    came = from_behind(far, -4)
    rank2 = jnp.concatenate([from_behind(rank1, 2), rank1], axis=1)
    near = near + came.astype(F32)
    rank3 = jnp.concatenate([from_behind(rank2, 4), rank2], axis=1)
    came = from_behind(near[:, :256], -2)
    near = near[:, 256:] + came
    came = from_behind(near[:, :128], -1)
    ups = [
        plain(
            functools.partial(mixed_kernel, first),
            "mixed",
            jax.ShapeDtypeStruct((ADAPTER_RANK, 2 * HEAD_SIZE), F32),
            w3,
            w2,
            w1,
            w0,
            scale,
            rank3,
            output_gradient,
        )
        for first in (0, 2)
    ]
    key_grad = (near[:, 128:] + came).astype(BF16)

    shares = plain(
        shares_kernel,
        "shares",
        jax.ShapeDtypeStruct((2, ADAPTER_RANK, LANES), BF16),
        key_grad,
        hidden,
        *ups,
    )
    shares = exchange(shares.reshape(N_DP, 8, LANES), "dp")
    shares = plain(
        fold_dp_kernel, "fold_dp", jax.ShapeDtypeStruct((N_FSDP, 8, 384), BF16), shares
    )
    shares = exchange(shares, "fsdp")
    shares = plain(
        fold_fsdp_kernel, "fold_fsdp", jax.ShapeDtypeStruct((N_DP, 8, 384), F32), shares
    )
    shares = exchange(shares, "dp")
    down, up = plain(
        spread_kernel,
        "spread",
        (
            jax.ShapeDtypeStruct((ADAPTER_RANK, 256), F32),
            jax.ShapeDtypeStruct((ADAPTER_RANK, KEY_HEADS * HEAD_SIZE), F32),
        ),
        shares,
    )
    return (down.T, up)


def solution(mesh):
    in_specs = (
        P(("dp", "fsdp"), None),
        P(("dp", "fsdp"), None),
        P(("dp", "fsdp"), None),
        P("dp", "fsdp"),
        P("fsdp", None),
        P(),
        P(("dp", "fsdp"), None),
    )
    out_specs = (P("fsdp", None), P())
    return jax.shard_map(local, mesh=mesh, in_specs=in_specs, out_specs=out_specs, check_vma=False)
```

```python
import functools
import math

import jax
import jax.numpy as jnp
from jax import lax
from jax.experimental import pallas as pl
from jax.experimental.pallas import tpu as pltpu
from jax.sharding import PartitionSpec as P

QUERY_HEADS = 32
KEY_HEADS = 4
HEAD_SIZE = 128
ADAPTER_RANK = 64
SPAN = 8
TOKENS = 128
WINDOW = SPAN * TOKENS
N_DP = 16
N_FSDP = 32
MODEL_WIDTH = 8192
GROUP = QUERY_HEADS // KEY_HEADS
COST = pl.CostEstimate(flops=10**10, bytes_accessed=2**27, transcendentals=0)
BF16 = jnp.bfloat16
F32 = jnp.float32
NT = (((1,), (1,)), ((), ()))


def whole(*arrays):
    return [pl.BlockSpec(memory_space=pltpu.VMEM) for _ in arrays]


def params(mebibytes):
    return pltpu.CompilerParams(vmem_limit_bytes=mebibytes * 1024 * 1024)


def from_behind(block, distance):
    route = [(i, i + distance) for i in range(N_FSDP) if 0 <= i + distance < N_FSDP]
    return lax.ppermute(block, "fsdp", route)


def exchange(slots, axis):
    return lax.all_to_all(slots, axis, 0, 0, tiled=True)


def lowrank_kernel(weight_ref, hidden_ref, out_ref):
    total = jnp.zeros((ADAPTER_RANK, TOKENS), F32)
    for f in range(N_FSDP):
        rows = jnp.concatenate(
            [weight_ref[half, :, f * 128 : f * 128 + 128] for half in range(2)], axis=1
        )
        total += lax.dot_general(
            rows, hidden_ref[:, f * 256 : f * 256 + 256], NT, preferred_element_type=F32
        )
    out_ref[...] = total.astype(BF16)


def score_pair(query_ref, keys, bias_ref, rows, weights_ref, stats_ref, at):
    factor = math.log2(math.e) / math.sqrt(HEAD_SIZE)
    for m in range(GROUP):
        lanes = slice(m * 128, m * 128 + 128)
        scores = lax.dot_general(keys, query_ref[:, lanes], NT, preferred_element_type=F32)
        scores = scores + bias_ref[rows, :]
        top = jnp.maximum(jnp.max(scores, axis=0, keepdims=True), -1e30) * factor
        weights = jnp.exp2(scores * factor - top)
        stats_ref[at : at + 1, lanes] = top
        stats_ref[at + 1 : at + 2, lanes] = jnp.sum(weights, axis=0, keepdims=True)
        weights_ref[:, lanes] = weights.astype(BF16)


def score_kernel(
    query_ref,
    keys2_ref,
    keys1_ref,
    keys0_ref,
    bias_ref,
    w2_ref,
    w1_ref,
    w0_ref,
    stats_ref,
):
    refs = ((keys2_ref, w2_ref), (keys1_ref, w1_ref), (keys0_ref, w0_ref))
    for i, (keys_ref, w_ref) in enumerate(refs):
        rows = slice(256 + i * 256, 512 + i * 256)
        score_pair(query_ref, keys_ref[...], bias_ref, rows, w_ref, stats_ref, 2 * i)
    stats_ref[6:8, :] = jnp.zeros((2, GROUP * TOKENS), F32)


def last_score_kernel(query_ref, keys_ref, bias_ref, weights_ref, stats_ref):
    def key_head(g, carry):
        keys = keys_ref[:, pl.ds(pl.multiple_of(g * HEAD_SIZE, HEAD_SIZE), HEAD_SIZE)]
        lanes = pl.ds(pl.multiple_of(g * GROUP * 128, 128), GROUP * 128)
        score_pair(
            query_ref.at[:, lanes],
            keys,
            bias_ref,
            slice(0, 256),
            weights_ref.at[:, lanes],
            stats_ref.at[:, lanes],
            0,
        )
        return carry

    lax.fori_loop(0, KEY_HEADS, key_head, 0)


def reached_kernel(gradient_ref, up_ref, out_ref):
    def key_head(g, carry):
        up = up_ref[:, pl.ds(pl.multiple_of(g * HEAD_SIZE, HEAD_SIZE), HEAD_SIZE)]
        for m in range(GROUP):
            lanes = pl.ds(pl.multiple_of((g * GROUP + m) * 128, 128), 128)
            out_ref[:, lanes] = lax.dot_general(
                up, gradient_ref[:, lanes], NT, preferred_element_type=F32
            ).astype(BF16)
        return carry

    lax.fori_loop(0, KEY_HEADS, key_head, 0)


def sums_of(weights_ref, scale, reached):
    shares = (reached * scale).astype(BF16)
    return lax.dot_general(weights_ref[...], shares, NT, preferred_element_type=F32).T


def far_kernel(w3_ref, w2_ref, last_ref, stats_ref, reached_ref, far_ref, scale_ref):
    stats = [last_ref[...]] + [stats_ref[2 * i : 2 * i + 2, :] for i in range(3)]
    top = stats[0][0:1]
    for s in stats[1:]:
        top = jnp.maximum(top, s[0:1])
    parts = [jnp.exp2(s[0:1] - top) for s in stats]
    inverse = 1.0 / sum(part * s[1:2] for part, s in zip(parts, stats))
    scales = [part * inverse for part in parts]
    for i, scale in enumerate(scales):
        scale_ref[i : i + 1, :] = scale
    reached = reached_ref[...].astype(F32)
    far_ref[:, :256] = sums_of(w3_ref, scales[0], reached).astype(BF16)
    far_ref[:, 256:] = sums_of(w2_ref, scales[1], reached).astype(BF16)


def near_kernel(w1_ref, w0_ref, scale_ref, reached_ref, near_ref):
    reached = reached_ref[...].astype(F32)
    near_ref[:, :256] = sums_of(w1_ref, scale_ref[2:3, :], reached)
    near_ref[:, 256:] = sums_of(w0_ref, scale_ref[3:4, :], reached)


def mixed_kernel(first, w3_ref, w2_ref, w1_ref, w0_ref, scale_ref, rank_ref, gradient_ref, out_ref):
    for g in range(2):
        share = jnp.zeros((ADAPTER_RANK, HEAD_SIZE), F32)
        for m in range(QUERY_HEADS // KEY_HEADS):
            h = (first + g) * 8 + m
            lanes = slice(h * 128, h * 128 + 128)
            mixed = jnp.zeros((ADAPTER_RANK, TOKENS), F32)
            for i, ref in enumerate((w3_ref, w2_ref, w1_ref, w0_ref)):
                rank = rank_ref[:, i * 256 : i * 256 + 256]
                part = jnp.dot(rank, ref[:, lanes], preferred_element_type=F32)
                mixed += part * scale_ref[i : i + 1, lanes]
            share += jnp.dot(
                mixed.astype(BF16), gradient_ref[:, lanes], preferred_element_type=F32
            )
        out_ref[:, g * 128 : g * 128 + 128] = share


DOWN = N_FSDP * 128
LANES = DOWN + 256


def shares_kernel(core_ref, key_ref, hidden_ref, up0_ref, up1_ref, own_ref, other_ref):
    for core in range(2):

        @pl.when(core_ref[0] == core)
        def _(core=core):
            halves = (own_ref, other_ref) if core == 0 else (other_ref, own_ref)
            for f in range(N_FSDP):
                product = jnp.dot(
                    key_ref[...], hidden_ref[:, f * 256 : f * 256 + 256], preferred_element_type=F32
                )
                for half, ref in enumerate(halves):
                    ref[:, f * 128 : f * 128 + 128] = product[:, half * 128 : half * 128 + 128]
            halves[0][:, DOWN:] = up0_ref[...]
            halves[1][:, DOWN:] = up1_ref[...]


def add_kernel(own_ref, other_ref, out_ref):
    for part in range(8):
        rows = slice(part * 8, part * 8 + 8)
        out_ref[part] = (own_ref[rows, :] + other_ref[rows, :]).astype(BF16)


def fold_dp_kernel(in_ref, out_ref):
    def total(columns):
        return sum(in_ref[d, :, columns].astype(F32) for d in range(N_DP // 2))

    up = total(slice(DOWN, LANES)).astype(BF16)
    for f in range(N_FSDP):
        out_ref[f, :, :128] = total(slice(f * 128, f * 128 + 128)).astype(BF16)
        out_ref[f, :, 128:] = up


def fold_fsdp_kernel(in_ref, out_ref):
    total = sum(in_ref[f].astype(F32) for f in range(N_FSDP))
    for d in range(N_DP):
        out_ref[d] = total


def spread_kernel(in_ref, down_ref, up_ref):
    for half in range(2):
        for part in range(8):
            rows = slice(part * 8, part * 8 + 8)
            block = in_ref[part * 2 + half]
            down_ref[rows, half * 128 : half * 128 + 128] = block[:, :128]
            up_ref[rows, half * 256 : half * 256 + 256] = block[:, 128:]


def plain(kernel, name, out_shape, *arrays):
    return pl.pallas_call(
        kernel,
        in_specs=whole(*arrays),
        out_specs=jax.tree.map(lambda _: pl.BlockSpec(memory_space=pltpu.VMEM), out_shape),
        out_shape=out_shape,
        compiler_params=params(20),
        cost_estimate=COST,
        name=name,
    )(*arrays)


def by_steps(kernel, name, steps, out_specs, out_shape, given, scratch=()):
    return pl.pallas_call(
        kernel,
        grid=(steps,),
        in_specs=[spec for spec, _ in given],
        out_specs=out_specs,
        out_shape=out_shape,
        scratch_shapes=list(scratch),
        compiler_params=params(60),
        cost_estimate=COST,
        name=name,
    )(*[array for _, array in given])


def columns(rows, lanes, first=0):
    return pl.BlockSpec((rows, lanes), lambda g: (0, first + g))


def fixed(*shape):
    return pl.BlockSpec(shape, lambda g: (0,) * len(shape))


def local(
    hidden, queries, keys, document_numbers, adapter_down_weight, adapter_up_weight, output_gradient
):
    position = lax.axis_index("fsdp")
    member = lax.axis_index("dp")
    half, part = member // 8, member % 8

    keys1, keys2, keys3 = [from_behind(keys, distance) for distance in (1, 2, 3)]
    weight_slice = lax.dynamic_slice(adapter_down_weight.T, (part * 8, half * 128), (8, 128))
    docs_row = document_numbers.reshape(1, TOKENS).astype(BF16)
    slot = jnp.concatenate([weight_slice, docs_row, jnp.zeros((7, 128), BF16)], axis=0)
    slots = jnp.broadcast_to(slot[None], (N_FSDP, 16, 128))
    row_parts = exchange(slots, "fsdp")
    pair0 = jnp.concatenate([keys1, keys], axis=0)
    pair1 = jnp.concatenate([keys3, keys2], axis=0)
    pair2 = from_behind(pair1, 2)
    weight_part = row_parts[:, :8].transpose(1, 0, 2).reshape(1, 8, DOWN)
    docs = row_parts[:, 8].astype(jnp.int32)
    weight_slots = jnp.broadcast_to(weight_part, (N_DP, 8, DOWN))
    weight = exchange(weight_slots, "dp").reshape(2, ADAPTER_RANK, DOWN)
    pair2 = lax.optimization_barrier((pair2, weight_slots))[0]
    pair3 = from_behind(pair2, 2)

    padded = jnp.concatenate([jnp.full((SPAN - 1, TOKENS), -1, jnp.int32), docs], axis=0)
    window_docs = lax.dynamic_slice(padded, (position, 0), (SPAN, TOKENS)).reshape(WINDOW)
    own_docs = document_numbers.reshape(TOKENS)
    key_pos = jnp.arange(WINDOW, dtype=jnp.int32) - (SPAN - 1) * TOKENS
    visible = (window_docs[:, None] == own_docs[None, :]) & (
        key_pos[:, None] <= jnp.arange(TOKENS, dtype=jnp.int32)[None, :]
    )
    bias = jnp.where(visible, 0.0, -jnp.inf).astype(F32)
    lanes = GROUP * TOKENS
    columns_of = QUERY_HEADS * TOKENS
    queries_by, keys_by, weights_by = columns(TOKENS, lanes), columns(256, 128), columns(256, lanes)
    weights_shape = jax.ShapeDtypeStruct((2 * TOKENS, columns_of), BF16)
    w2, w1, w0, stats = by_steps(
        score_kernel,
        "score",
        KEY_HEADS,
        [weights_by] * 3 + [columns(8, lanes)],
        [weights_shape] * 3 + [jax.ShapeDtypeStruct((8, columns_of), F32)],
        [
            (queries_by, queries),
            (keys_by, pair2),
            (keys_by, pair1),
            (keys_by, pair0),
            (fixed(WINDOW, TOKENS), bias),
        ],
    )
    reached = plain(
        reached_kernel,
        "reached",
        jax.ShapeDtypeStruct((ADAPTER_RANK, columns_of), BF16),
        output_gradient,
        lax.optimization_barrier((adapter_up_weight, stats))[0],
    )
    rank = plain(
        lowrank_kernel, "lowrank", jax.ShapeDtypeStruct((ADAPTER_RANK, TOKENS), BF16), weight, hidden
    )
    rank1 = jnp.concatenate([from_behind(rank, 1), rank], axis=1)
    pair3, rank1, stats = lax.optimization_barrier((pair3, rank1, stats))
    rank2 = jnp.concatenate([from_behind(rank1, 2), rank1], axis=1)
    w3, last = plain(
        last_score_kernel,
        "last_score",
        (weights_shape, jax.ShapeDtypeStruct((2, columns_of), F32)),
        queries,
        pair3,
        bias[:256],
    )
    w3, rank2 = lax.optimization_barrier((w3, rank2))
    far, scale = plain(
        far_kernel,
        "far",
        (
            jax.ShapeDtypeStruct((ADAPTER_RANK, WINDOW // 2), BF16),
            jax.ShapeDtypeStruct((4, columns_of), F32),
        ),
        w3,
        w2,
        last,
        stats,
        reached,
    )
    near = plain(
        near_kernel,
        "near",
        jax.ShapeDtypeStruct((ADAPTER_RANK, WINDOW // 2), F32),
        w1,
        w0,
        scale,
        reached,
    )
    came = from_behind(far, -4)
    near = near + came.astype(F32)
    rank3 = jnp.concatenate([from_behind(rank2, 4), rank2], axis=1)
    came = from_behind(near[:, :256], -2)
    near = near[:, 256:] + came
    came = from_behind(near[:, :128], -1)
    ups = [
        plain(
            functools.partial(mixed_kernel, first),
            "mixed",
            jax.ShapeDtypeStruct((ADAPTER_RANK, 2 * HEAD_SIZE), F32),
            w3,
            w2,
            w1,
            w0,
            scale,
            rank3,
            output_gradient,
        )
        for first in (0, 2)
    ]
    key_grad = (near[:, 128:] + came).astype(BF16)

    share = jax.ShapeDtypeStruct((ADAPTER_RANK, LANES), F32)
    own, other = pl.pallas_call(
        shares_kernel,
        in_specs=[pl.BlockSpec(memory_space=pltpu.SMEM)] + whole(key_grad, hidden, *ups),
        out_specs=whole(share, share),
        out_shape=(share, share),
        compiler_params=params(20),
        cost_estimate=COST,
        name="shares",
    )((member % 2).astype(jnp.int32).reshape(1), key_grad, hidden, *ups)
    other = lax.ppermute(other, "dp", [(d, d ^ 1) for d in range(N_DP)])
    shares = plain(
        add_kernel, "add", jax.ShapeDtypeStruct((N_DP // 2, 8, LANES), BF16), own, other
    )
    groups = [list(range(core, N_DP, 2)) for core in range(2)]
    shares = lax.all_to_all(shares, "dp", 0, 0, axis_index_groups=groups, tiled=True)
    shares = plain(
        fold_dp_kernel, "fold_dp", jax.ShapeDtypeStruct((N_FSDP, 8, 384), BF16), shares
    )
    shares = exchange(shares, "fsdp")
    shares = plain(
        fold_fsdp_kernel, "fold_fsdp", jax.ShapeDtypeStruct((N_DP, 8, 384), F32), shares
    )
    shares = exchange(shares, "dp")
    down, up = plain(
        spread_kernel,
        "spread",
        (
            jax.ShapeDtypeStruct((ADAPTER_RANK, 256), F32),
            jax.ShapeDtypeStruct((ADAPTER_RANK, KEY_HEADS * HEAD_SIZE), F32),
        ),
        shares,
    )
    return (down.T, up)


def solution(mesh):
    in_specs = (
        P(("dp", "fsdp"), None),
        P(("dp", "fsdp"), None),
        P(("dp", "fsdp"), None),
        P("dp", "fsdp"),
        P("fsdp", None),
        P(),
        P(("dp", "fsdp"), None),
    )
    out_specs = (P("fsdp", None), P())
    return jax.shard_map(local, mesh=mesh, in_specs=in_specs, out_specs=out_specs, check_vma=False)
```

```python
import functools
import math

import jax
import jax.numpy as jnp
from jax import lax
from jax.experimental import pallas as pl
from jax.experimental.pallas import tpu as pltpu
from jax.sharding import PartitionSpec as P

QUERY_HEADS = 32
KEY_HEADS = 4
HEAD_SIZE = 128
ADAPTER_RANK = 64
SPAN = 8
TOKENS = 128
WINDOW = SPAN * TOKENS
N_DP = 16
N_FSDP = 32
MODEL_WIDTH = 8192
GROUP = QUERY_HEADS // KEY_HEADS
COST = pl.CostEstimate(flops=10**10, bytes_accessed=2**27, transcendentals=0)
BF16 = jnp.bfloat16
F32 = jnp.float32
NT = (((1,), (1,)), ((), ()))


def whole(*arrays):
    return [pl.BlockSpec(memory_space=pltpu.VMEM) for _ in arrays]


def params(mebibytes):
    return pltpu.CompilerParams(vmem_limit_bytes=mebibytes * 1024 * 1024)


def from_behind(block, distance):
    route = [(i, i + distance) for i in range(N_FSDP) if 0 <= i + distance < N_FSDP]
    return lax.ppermute(block, "fsdp", route)


def exchange(slots, axis):
    return lax.all_to_all(slots, axis, 0, 0, tiled=True)


def docs_kernel(in_ref, out_ref):
    out_ref[...] = in_ref[...]


def lowrank_kernel(weight_ref, hidden_ref, out_ref):
    total = jnp.zeros((ADAPTER_RANK, TOKENS), F32)
    for f in range(N_FSDP):
        rows = jnp.concatenate(
            [weight_ref[half, :, f * 128 : f * 128 + 128] for half in range(2)], axis=1
        )
        total += lax.dot_general(
            rows, hidden_ref[:, f * 256 : f * 256 + 256], NT, preferred_element_type=F32
        )
    out_ref[...] = total.astype(BF16)


def score_pair(query_ref, keys, bias_ref, rows, weights_ref, stats_ref, at):
    factor = math.log2(math.e) / math.sqrt(HEAD_SIZE)
    for m in range(GROUP):
        lanes = slice(m * 128, m * 128 + 128)
        scores = lax.dot_general(keys, query_ref[:, lanes], NT, preferred_element_type=F32)
        scores = scores + bias_ref[rows, :]
        top = jnp.maximum(jnp.max(scores, axis=0, keepdims=True), -1e30) * factor
        weights = jnp.exp2(scores * factor - top)
        stats_ref[at : at + 1, lanes] = top
        stats_ref[at + 1 : at + 2, lanes] = jnp.sum(weights, axis=0, keepdims=True)
        weights_ref[:, lanes] = weights.astype(BF16)


def score_kernel(
    query_ref,
    keys2_ref,
    keys1_ref,
    keys0_ref,
    bias_ref,
    w2_ref,
    w1_ref,
    w0_ref,
    stats_ref,
):
    refs = ((keys2_ref, w2_ref), (keys1_ref, w1_ref), (keys0_ref, w0_ref))
    for i, (keys_ref, w_ref) in enumerate(refs):
        rows = slice(256 + i * 256, 512 + i * 256)
        score_pair(query_ref, keys_ref[...], bias_ref, rows, w_ref, stats_ref, 2 * i)
    stats_ref[6:8, :] = jnp.zeros((2, GROUP * TOKENS), F32)


def last_score_kernel(query_ref, keys_ref, bias_ref, weights_ref, stats_ref):
    def key_head(g, carry):
        keys = keys_ref[:, pl.ds(pl.multiple_of(g * HEAD_SIZE, HEAD_SIZE), HEAD_SIZE)]
        lanes = pl.ds(pl.multiple_of(g * GROUP * 128, 128), GROUP * 128)
        score_pair(
            query_ref.at[:, lanes],
            keys,
            bias_ref,
            slice(0, 256),
            weights_ref.at[:, lanes],
            stats_ref.at[:, lanes],
            0,
        )
        return carry

    lax.fori_loop(0, KEY_HEADS, key_head, 0)


def reached_kernel(gradient_ref, up_ref, out_ref):
    def key_head(g, carry):
        up = up_ref[:, pl.ds(pl.multiple_of(g * HEAD_SIZE, HEAD_SIZE), HEAD_SIZE)]
        for m in range(GROUP):
            lanes = pl.ds(pl.multiple_of((g * GROUP + m) * 128, 128), 128)
            out_ref[:, lanes] = lax.dot_general(
                up, gradient_ref[:, lanes], NT, preferred_element_type=F32
            ).astype(BF16)
        return carry

    lax.fori_loop(0, KEY_HEADS, key_head, 0)


def sums_of(weights_ref, scale, reached):
    shares = (reached * scale).astype(BF16)
    return lax.dot_general(weights_ref[...], shares, NT, preferred_element_type=F32).T


def far_kernel(w3_ref, w2_ref, last_ref, stats_ref, reached_ref, far_ref, scale_ref):
    stats = [last_ref[...]] + [stats_ref[2 * i : 2 * i + 2, :] for i in range(3)]
    top = stats[0][0:1]
    for s in stats[1:]:
        top = jnp.maximum(top, s[0:1])
    parts = [jnp.exp2(s[0:1] - top) for s in stats]
    inverse = 1.0 / sum(part * s[1:2] for part, s in zip(parts, stats))
    scales = [part * inverse for part in parts]
    for i, scale in enumerate(scales):
        scale_ref[i : i + 1, :] = scale
    reached = reached_ref[...].astype(F32)
    far_ref[:, :256] = sums_of(w3_ref, scales[0], reached).astype(BF16)
    far_ref[:, 256:] = sums_of(w2_ref, scales[1], reached).astype(BF16)


def near_kernel(w1_ref, w0_ref, scale_ref, reached_ref, near_ref):
    reached = reached_ref[...].astype(F32)
    near_ref[:, :256] = sums_of(w1_ref, scale_ref[2:3, :], reached)
    near_ref[:, 256:] = sums_of(w0_ref, scale_ref[3:4, :], reached)


def mixed_kernel(first, w3_ref, w2_ref, w1_ref, w0_ref, scale_ref, rank_ref, gradient_ref, out_ref):
    for g in range(2):
        share = jnp.zeros((ADAPTER_RANK, HEAD_SIZE), F32)
        for m in range(QUERY_HEADS // KEY_HEADS):
            h = (first + g) * 8 + m
            lanes = slice(h * 128, h * 128 + 128)
            mixed = jnp.zeros((ADAPTER_RANK, TOKENS), F32)
            for i, ref in enumerate((w3_ref, w2_ref, w1_ref, w0_ref)):
                rank = rank_ref[:, i * 256 : i * 256 + 256]
                part = jnp.dot(rank, ref[:, lanes], preferred_element_type=F32)
                mixed += part * scale_ref[i : i + 1, lanes]
            share += jnp.dot(
                mixed.astype(BF16), gradient_ref[:, lanes], preferred_element_type=F32
            )
        out_ref[:, g * 128 : g * 128 + 128] = share


DOWN = N_FSDP * 128
LANES = DOWN + 256


def shares_kernel(key_ref, hidden_ref, up0_ref, up1_ref, out_ref):
    for f in range(N_FSDP):
        product = jnp.dot(
            key_ref[...], hidden_ref[:, f * 256 : f * 256 + 256], preferred_element_type=F32
        ).astype(BF16)
        for half in range(2):
            out_ref[half, :, f * 128 : f * 128 + 128] = product[:, half * 128 : half * 128 + 128]
    for half, up_ref in enumerate((up0_ref, up1_ref)):
        out_ref[half, :, DOWN:] = up_ref[...].astype(BF16)


def fold_dp_kernel(in_ref, out_ref):
    def total(columns):
        return sum(in_ref[d, :, columns].astype(F32) for d in range(N_DP))

    up = total(slice(DOWN, LANES)).astype(BF16)
    for f in range(N_FSDP):
        out_ref[f, :, :128] = total(slice(f * 128, f * 128 + 128)).astype(BF16)
        out_ref[f, :, 128:] = up


def fold_fsdp_kernel(in_ref, out_ref):
    total = sum(in_ref[f].astype(F32) for f in range(N_FSDP))
    for d in range(N_DP):
        out_ref[d] = total


def spread_kernel(in_ref, down_ref, up_ref):
    for half in range(2):
        for part in range(8):
            rows = slice(part * 8, part * 8 + 8)
            block = in_ref[half * 8 + part]
            down_ref[rows, half * 128 : half * 128 + 128] = block[:, :128]
            up_ref[rows, half * 256 : half * 256 + 256] = block[:, 128:]


def plain(kernel, name, out_shape, *arrays):
    return pl.pallas_call(
        kernel,
        in_specs=whole(*arrays),
        out_specs=jax.tree.map(lambda _: pl.BlockSpec(memory_space=pltpu.VMEM), out_shape),
        out_shape=out_shape,
        compiler_params=params(20),
        cost_estimate=COST,
        name=name,
    )(*arrays)


def by_steps(kernel, name, steps, out_specs, out_shape, given, scratch=()):
    return pl.pallas_call(
        kernel,
        grid=(steps,),
        in_specs=[spec for spec, _ in given],
        out_specs=out_specs,
        out_shape=out_shape,
        scratch_shapes=list(scratch),
        compiler_params=params(60),
        cost_estimate=COST,
        name=name,
    )(*[array for _, array in given])


def columns(rows, lanes, first=0):
    return pl.BlockSpec((rows, lanes), lambda g: (0, first + g))


def fixed(*shape):
    return pl.BlockSpec(shape, lambda g: (0,) * len(shape))


def local(
    hidden, queries, keys, document_numbers, adapter_down_weight, adapter_up_weight, output_gradient
):
    position = lax.axis_index("fsdp")
    member = lax.axis_index("dp")
    half, part = member // 8, member % 8

    keys1, keys2, keys3 = [from_behind(keys, distance) for distance in (1, 2, 3)]
    weight_slice = lax.dynamic_slice(adapter_down_weight.T, (part * 8, half * 128), (8, 128))
    slot = jnp.concatenate(
        [
            weight_slice,
            document_numbers.reshape(1, TOKENS).astype(BF16),
            jnp.zeros((7, 128), BF16),
        ],
        axis=0,
    )
    docs_row = plain(
        docs_kernel, "docs", jax.ShapeDtypeStruct((1, TOKENS), jnp.int32), document_numbers
    )
    slots = jnp.broadcast_to(slot[None], (N_FSDP, 16, 128))
    row_parts = exchange(slots, "fsdp")
    pair0 = jnp.concatenate([keys1, keys], axis=0)
    pair1 = jnp.concatenate([keys3, keys2], axis=0)
    pair2 = from_behind(pair1, 2)
    weight_part = row_parts[:, :8].transpose(1, 0, 2).reshape(1, 8, DOWN)
    docs = row_parts[:, 8].astype(jnp.int32)
    weight_slots = jnp.broadcast_to(weight_part, (N_DP, 8, DOWN))
    weight = exchange(weight_slots, "dp").reshape(2, ADAPTER_RANK, DOWN)
    pair2 = lax.optimization_barrier((pair2, weight_slots))[0]
    pair3 = from_behind(pair2, 2)

    padded = jnp.concatenate([jnp.full((SPAN - 1, TOKENS), -1, jnp.int32), docs], axis=0)
    window_docs = lax.dynamic_slice(padded, (position, 0), (SPAN, TOKENS)).reshape(WINDOW)
    own_docs = docs_row[0]
    key_pos = jnp.arange(WINDOW, dtype=jnp.int32) - (SPAN - 1) * TOKENS
    visible = (window_docs[:, None] == own_docs[None, :]) & (
        key_pos[:, None] <= jnp.arange(TOKENS, dtype=jnp.int32)[None, :]
    )
    bias = jnp.where(visible, 0.0, -jnp.inf).astype(F32)
    lanes = GROUP * TOKENS
    columns_of = QUERY_HEADS * TOKENS
    queries_by, keys_by, weights_by = columns(TOKENS, lanes), columns(256, 128), columns(256, lanes)
    weights_shape = jax.ShapeDtypeStruct((2 * TOKENS, columns_of), BF16)
    w2, w1, w0, stats = by_steps(
        score_kernel,
        "score",
        KEY_HEADS,
        [weights_by] * 3 + [columns(8, lanes)],
        [weights_shape] * 3 + [jax.ShapeDtypeStruct((8, columns_of), F32)],
        [
            (queries_by, queries),
            (keys_by, pair2),
            (keys_by, pair1),
            (keys_by, pair0),
            (fixed(WINDOW, TOKENS), bias),
        ],
    )
    reached = plain(
        reached_kernel,
        "reached",
        jax.ShapeDtypeStruct((ADAPTER_RANK, columns_of), BF16),
        output_gradient,
        lax.optimization_barrier((adapter_up_weight, stats))[0],
    )
    rank = plain(
        lowrank_kernel, "lowrank", jax.ShapeDtypeStruct((ADAPTER_RANK, TOKENS), BF16), weight, hidden
    )
    rank1 = jnp.concatenate([from_behind(rank, 1), rank], axis=1)
    pair3, rank1, stats = lax.optimization_barrier((pair3, rank1, stats))
    rank2 = jnp.concatenate([from_behind(rank1, 2), rank1], axis=1)
    w3, last = plain(
        last_score_kernel,
        "last_score",
        (weights_shape, jax.ShapeDtypeStruct((2, columns_of), F32)),
        queries,
        pair3,
        bias,
    )
    w3, rank2 = lax.optimization_barrier((w3, rank2))
    far, scale = plain(
        far_kernel,
        "far",
        (
            jax.ShapeDtypeStruct((ADAPTER_RANK, WINDOW // 2), BF16),
            jax.ShapeDtypeStruct((4, columns_of), F32),
        ),
        w3,
        w2,
        last,
        stats,
        reached,
    )
    near = plain(
        near_kernel,
        "near",
        jax.ShapeDtypeStruct((ADAPTER_RANK, WINDOW // 2), F32),
        w1,
        w0,
        scale,
        reached,
    )
    came = from_behind(far, -4)
    near = near + came.astype(F32)
    rank3 = jnp.concatenate([from_behind(rank2, 4), rank2], axis=1)
    came = from_behind(near[:, :256], -2)
    near = near[:, 256:] + came
    came = from_behind(near[:, :128], -1)
    ups = [
        plain(
            functools.partial(mixed_kernel, first),
            "mixed",
            jax.ShapeDtypeStruct((ADAPTER_RANK, 2 * HEAD_SIZE), F32),
            w3,
            w2,
            w1,
            w0,
            scale,
            rank3,
            output_gradient,
        )
        for first in (0, 2)
    ]
    key_grad = (near[:, 128:] + came).astype(BF16)

    shares = plain(
        shares_kernel,
        "shares",
        jax.ShapeDtypeStruct((2, ADAPTER_RANK, LANES), BF16),
        key_grad,
        hidden,
        *ups,
    )
    shares = exchange(shares.reshape(N_DP, 8, LANES), "dp")
    shares = plain(
        fold_dp_kernel, "fold_dp", jax.ShapeDtypeStruct((N_FSDP, 8, 384), BF16), shares
    )
    shares = exchange(shares, "fsdp")
    shares = plain(
        fold_fsdp_kernel, "fold_fsdp", jax.ShapeDtypeStruct((N_DP, 8, 384), F32), shares
    )
    shares = exchange(shares, "dp")
    down, up = plain(
        spread_kernel,
        "spread",
        (
            jax.ShapeDtypeStruct((ADAPTER_RANK, 256), F32),
            jax.ShapeDtypeStruct((ADAPTER_RANK, KEY_HEADS * HEAD_SIZE), F32),
        ),
        shares,
    )
    return (down.T, up)


def solution(mesh):
    in_specs = (
        P(("dp", "fsdp"), None),
        P(("dp", "fsdp"), None),
        P(("dp", "fsdp"), None),
        P("dp", "fsdp"),
        P("fsdp", None),
        P(),
        P(("dp", "fsdp"), None),
    )
    out_specs = (P("fsdp", None), P())
    return jax.shard_map(local, mesh=mesh, in_specs=in_specs, out_specs=out_specs, check_vma=False)
```

```python
import functools
import math

import jax
import jax.numpy as jnp
from jax import lax
from jax.experimental import pallas as pl
from jax.experimental.pallas import tpu as pltpu
from jax.sharding import PartitionSpec as P

QUERY_HEADS = 32
KEY_HEADS = 4
HEAD_SIZE = 128
ADAPTER_RANK = 64
SPAN = 8
TOKENS = 128
WINDOW = SPAN * TOKENS
N_DP = 16
N_FSDP = 32
MODEL_WIDTH = 8192
GROUP = QUERY_HEADS // KEY_HEADS
ORDER = (7, 3, 5, 1, 6, 2, 4, 0)
COST = pl.CostEstimate(flops=10**10, bytes_accessed=2**27, transcendentals=0)
BF16 = jnp.bfloat16
F32 = jnp.float32
NT = (((1,), (1,)), ((), ()))


def whole(*arrays):
    return [pl.BlockSpec(memory_space=pltpu.VMEM) for _ in arrays]


def params(mebibytes):
    return pltpu.CompilerParams(vmem_limit_bytes=mebibytes * 1024 * 1024)


def from_behind(block, distance):
    route = [(i, i + distance) for i in range(N_FSDP) if 0 <= i + distance < N_FSDP]
    return lax.ppermute(block, "fsdp", route)


def exchange(slots, axis):
    return lax.all_to_all(slots, axis, 0, 0, tiled=True)


def docs_kernel(in_ref, out_ref):
    out_ref[...] = in_ref[...]


def lowrank_kernel(weight_ref, hidden_ref, out_ref):
    total = jnp.zeros((ADAPTER_RANK, TOKENS), F32)
    for f in range(N_FSDP):
        rows = jnp.concatenate(
            [weight_ref[half, :, f * 128 : f * 128 + 128] for half in range(2)], axis=1
        )
        total += lax.dot_general(
            rows, hidden_ref[:, f * 256 : f * 256 + 256], NT, preferred_element_type=F32
        )
    out_ref[...] = total.astype(BF16)


def score_pair(query_ref, keys, bias_ref, rows, weights_ref, stats_ref, at):
    factor = math.log2(math.e) / math.sqrt(HEAD_SIZE)
    for m in range(GROUP):
        lanes = slice(m * 128, m * 128 + 128)
        scores = lax.dot_general(keys, query_ref[:, lanes], NT, preferred_element_type=F32)
        scores = scores + bias_ref[rows, :]
        top = jnp.maximum(jnp.max(scores, axis=0, keepdims=True), -1e30) * factor
        weights = jnp.exp2(scores * factor - top)
        stats_ref[at : at + 1, lanes] = top
        stats_ref[at + 1 : at + 2, lanes] = jnp.sum(weights, axis=0, keepdims=True)
        weights_ref[:, lanes] = weights.astype(BF16)


def score_kernel(
    query_ref, keys1_ref, keys0_ref, bias_ref, w1_ref, w0_ref, stats_ref
):
    for i, (keys_ref, w_ref) in enumerate(((keys1_ref, w1_ref), (keys0_ref, w0_ref))):
        rows = slice(512 + i * 256, 768 + i * 256)
        score_pair(query_ref, keys_ref[...], bias_ref, rows, w_ref, stats_ref, 2 * i)
    stats_ref[4:8, :] = jnp.zeros((4, GROUP * TOKENS), F32)


def last_score_kernel(query_ref, keys_ref, bias_ref, w3_ref, w2_ref, stats_ref):
    def key_head(g, carry):
        keys = keys_ref[:, pl.ds(pl.multiple_of(g * HEAD_SIZE, HEAD_SIZE), HEAD_SIZE)]
        lanes = pl.ds(pl.multiple_of(g * GROUP * 128, 128), GROUP * 128)
        for i, w_ref in enumerate((w3_ref, w2_ref)):
            rows = slice(i * 256, i * 256 + 256)
            score_pair(
                query_ref.at[:, lanes],
                keys[rows],
                bias_ref,
                rows,
                w_ref.at[:, lanes],
                stats_ref.at[:, lanes],
                2 * i,
            )
        return carry

    lax.fori_loop(0, KEY_HEADS, key_head, 0)


def reached_kernel(gradient_ref, up_ref, out_ref):
    def key_head(g, carry):
        up = up_ref[:, pl.ds(pl.multiple_of(g * HEAD_SIZE, HEAD_SIZE), HEAD_SIZE)]
        for m in range(GROUP):
            lanes = pl.ds(pl.multiple_of((g * GROUP + m) * 128, 128), 128)
            out_ref[:, lanes] = lax.dot_general(
                up, gradient_ref[:, lanes], NT, preferred_element_type=F32
            ).astype(BF16)
        return carry

    lax.fori_loop(0, KEY_HEADS, key_head, 0)


def sums_of(weights_ref, scale, reached):
    shares = (reached * scale).astype(BF16)
    return lax.dot_general(weights_ref[...], shares, NT, preferred_element_type=F32).T


def far_kernel(w3_ref, w2_ref, last_ref, stats_ref, reached_ref, far_ref, scale_ref):
    stats = [ref[2 * i : 2 * i + 2, :] for ref in (last_ref, stats_ref) for i in range(2)]
    top = stats[0][0:1]
    for s in stats[1:]:
        top = jnp.maximum(top, s[0:1])
    parts = [jnp.exp2(s[0:1] - top) for s in stats]
    inverse = 1.0 / sum(part * s[1:2] for part, s in zip(parts, stats))
    scales = [part * inverse for part in parts]
    for i, scale in enumerate(scales):
        scale_ref[i : i + 1, :] = scale
    reached = reached_ref[...].astype(F32)
    far_ref[:, :256] = sums_of(w3_ref, scales[0], reached).astype(BF16)
    far_ref[:, 256:] = sums_of(w2_ref, scales[1], reached).astype(BF16)


def near_kernel(w1_ref, w0_ref, scale_ref, reached_ref, near_ref):
    reached = reached_ref[...].astype(F32)
    near_ref[:, :256] = sums_of(w1_ref, scale_ref[2:3, :], reached)
    near_ref[:, 256:] = sums_of(w0_ref, scale_ref[3:4, :], reached)


def mixed_kernel(first, w3_ref, w2_ref, w1_ref, w0_ref, scale_ref, rank_ref, gradient_ref, out_ref):
    for g in range(2):
        share = jnp.zeros((ADAPTER_RANK, HEAD_SIZE), F32)
        for m in range(QUERY_HEADS // KEY_HEADS):
            h = (first + g) * 8 + m
            lanes = slice(h * 128, h * 128 + 128)
            mixed = jnp.zeros((ADAPTER_RANK, TOKENS), F32)
            for i, ref in enumerate((w3_ref, w2_ref, w1_ref, w0_ref)):
                rank = rank_ref[:, i * 256 : i * 256 + 256]
                part = jnp.dot(rank, ref[:, lanes], preferred_element_type=F32)
                mixed += part * scale_ref[i : i + 1, lanes]
            share += jnp.dot(
                mixed.astype(BF16), gradient_ref[:, lanes], preferred_element_type=F32
            )
        out_ref[:, g * 128 : g * 128 + 128] = share


DOWN = N_FSDP * 128
LANES = DOWN + 256


def shares_kernel(key_ref, hidden_ref, up0_ref, up1_ref, out_ref):
    for f in range(N_FSDP):
        product = jnp.dot(
            key_ref[...], hidden_ref[:, f * 256 : f * 256 + 256], preferred_element_type=F32
        ).astype(BF16)
        for half in range(2):
            out_ref[half, :, f * 128 : f * 128 + 128] = product[:, half * 128 : half * 128 + 128]
    for half, up_ref in enumerate((up0_ref, up1_ref)):
        out_ref[half, :, DOWN:] = up_ref[...].astype(BF16)


def fold_dp_kernel(in_ref, out_ref):
    def total(columns):
        return sum(in_ref[d, :, columns].astype(F32) for d in range(N_DP))

    up = total(slice(DOWN, LANES)).astype(BF16)
    for f in range(N_FSDP):
        out_ref[f, :, :128] = total(slice(f * 128, f * 128 + 128)).astype(BF16)
        out_ref[f, :, 128:] = up


def fold_fsdp_kernel(in_ref, out_ref):
    total = sum(in_ref[f].astype(F32) for f in range(N_FSDP))
    for d in range(N_DP):
        out_ref[d] = total


def spread_kernel(in_ref, down_ref, up_ref):
    for half in range(2):
        for part in range(8):
            rows = slice(part * 8, part * 8 + 8)
            block = in_ref[half * 8 + part]
            down_ref[rows, half * 128 : half * 128 + 128] = block[:, :128]
            up_ref[rows, half * 256 : half * 256 + 256] = block[:, 128:]


def plain(kernel, name, out_shape, *arrays):
    return pl.pallas_call(
        kernel,
        in_specs=whole(*arrays),
        out_specs=jax.tree.map(lambda _: pl.BlockSpec(memory_space=pltpu.VMEM), out_shape),
        out_shape=out_shape,
        compiler_params=params(20),
        cost_estimate=COST,
        name=name,
    )(*arrays)


def by_steps(kernel, name, steps, out_specs, out_shape, given, scratch=()):
    return pl.pallas_call(
        kernel,
        grid=(steps,),
        in_specs=[spec for spec, _ in given],
        out_specs=out_specs,
        out_shape=out_shape,
        scratch_shapes=list(scratch),
        compiler_params=params(60),
        cost_estimate=COST,
        name=name,
    )(*[array for _, array in given])


def columns(rows, lanes, first=0):
    return pl.BlockSpec((rows, lanes), lambda g: (0, first + g))


def fixed(*shape):
    return pl.BlockSpec(shape, lambda g: (0,) * len(shape))


def local(
    hidden, queries, keys, document_numbers, adapter_down_weight, adapter_up_weight, output_gradient
):
    position = lax.axis_index("fsdp")
    member = lax.axis_index("dp")
    half, part = member // 8, member % 8

    pair0 = jnp.concatenate([from_behind(keys, 4), keys], axis=0)
    pair1 = from_behind(pair0, 2)
    weight_slice = lax.dynamic_slice(adapter_down_weight.T, (part * 8, half * 128), (8, 128))
    slot = jnp.concatenate(
        [
            weight_slice,
            document_numbers.reshape(1, TOKENS).astype(BF16),
            jnp.zeros((7, 128), BF16),
        ],
        axis=0,
    )
    docs_row = plain(
        docs_kernel, "docs", jax.ShapeDtypeStruct((1, TOKENS), jnp.int32), document_numbers
    )
    slots = jnp.broadcast_to(slot[None], (N_FSDP, 16, 128))
    row_parts = exchange(slots, "fsdp")
    weight_part = row_parts[:, :8].transpose(1, 0, 2).reshape(1, 8, DOWN)
    docs = row_parts[:, 8].astype(jnp.int32)
    weight_slots = jnp.broadcast_to(weight_part, (N_DP, 8, DOWN))
    weight = exchange(weight_slots, "dp").reshape(2, ADAPTER_RANK, DOWN)
    pair1 = lax.optimization_barrier((pair1, weight_slots))[0]
    quad = from_behind(jnp.concatenate([pair1, pair0], axis=0), 1)

    padded = jnp.concatenate([jnp.full((SPAN - 1, TOKENS), -1, jnp.int32), docs], axis=0)
    window_docs = lax.dynamic_slice(padded, (position, 0), (SPAN, TOKENS))
    window_docs = jnp.concatenate([window_docs[7 - d : 8 - d] for d in ORDER]).reshape(WINDOW)
    own_docs = docs_row[0]
    key_pos = jnp.concatenate([jnp.arange(TOKENS, dtype=jnp.int32) - d * TOKENS for d in ORDER])
    visible = (window_docs[:, None] == own_docs[None, :]) & (
        key_pos[:, None] <= jnp.arange(TOKENS, dtype=jnp.int32)[None, :]
    )
    bias = jnp.where(visible, 0.0, -jnp.inf).astype(F32)
    lanes = GROUP * TOKENS
    columns_of = QUERY_HEADS * TOKENS
    queries_by, keys_by, weights_by = columns(TOKENS, lanes), columns(256, 128), columns(256, lanes)
    weights_shape = jax.ShapeDtypeStruct((2 * TOKENS, columns_of), BF16)
    w1, w0, stats = by_steps(
        score_kernel,
        "score",
        KEY_HEADS,
        [weights_by] * 2 + [columns(8, lanes)],
        [weights_shape] * 2 + [jax.ShapeDtypeStruct((8, columns_of), F32)],
        [
            (queries_by, queries),
            (keys_by, pair1),
            (keys_by, pair0),
            (fixed(WINDOW, TOKENS), bias),
        ],
    )
    reached = plain(
        reached_kernel,
        "reached",
        jax.ShapeDtypeStruct((ADAPTER_RANK, columns_of), BF16),
        output_gradient,
        lax.optimization_barrier((adapter_up_weight, stats))[0],
    )
    rank = plain(
        lowrank_kernel, "lowrank", jax.ShapeDtypeStruct((ADAPTER_RANK, TOKENS), BF16), weight, hidden
    )
    rank1 = jnp.concatenate([from_behind(rank, 4), rank], axis=1)
    quad, rank, stats = lax.optimization_barrier((quad, rank, stats))
    rank2 = jnp.concatenate([from_behind(rank1, 2), rank1], axis=1)
    w3, w2, last = plain(
        last_score_kernel,
        "last_score",
        (weights_shape, weights_shape, jax.ShapeDtypeStruct((4, columns_of), F32)),
        queries,
        quad,
        bias,
    )
    far, scale = plain(
        far_kernel,
        "far",
        (
            jax.ShapeDtypeStruct((ADAPTER_RANK, WINDOW // 2), BF16),
            jax.ShapeDtypeStruct((4, columns_of), F32),
        ),
        w3,
        w2,
        last,
        stats,
        reached,
    )
    near = plain(
        near_kernel,
        "near",
        jax.ShapeDtypeStruct((ADAPTER_RANK, WINDOW // 2), F32),
        w1,
        w0,
        scale,
        reached,
    )
    came = from_behind(far, -1)
    near = near + came.astype(F32)
    rank3 = jnp.concatenate([from_behind(rank2, 1), rank2], axis=1)
    came = from_behind(near[:, :256], -2)
    near = near[:, 256:] + came
    came = from_behind(near[:, :128], -4)
    ups = [
        plain(
            functools.partial(mixed_kernel, first),
            "mixed",
            jax.ShapeDtypeStruct((ADAPTER_RANK, 2 * HEAD_SIZE), F32),
            w3,
            w2,
            w1,
            w0,
            scale,
            rank3,
            output_gradient,
        )
        for first in (0, 2)
    ]
    key_grad = (near[:, 128:] + came).astype(BF16)

    shares = plain(
        shares_kernel,
        "shares",
        jax.ShapeDtypeStruct((2, ADAPTER_RANK, LANES), BF16),
        key_grad,
        hidden,
        *ups,
    )
    shares = exchange(shares.reshape(N_DP, 8, LANES), "dp")
    shares = plain(
        fold_dp_kernel, "fold_dp", jax.ShapeDtypeStruct((N_FSDP, 8, 384), BF16), shares
    )
    shares = exchange(shares, "fsdp")
    shares = plain(
        fold_fsdp_kernel, "fold_fsdp", jax.ShapeDtypeStruct((N_DP, 8, 384), F32), shares
    )
    shares = exchange(shares, "dp")
    down, up = plain(
        spread_kernel,
        "spread",
        (
            jax.ShapeDtypeStruct((ADAPTER_RANK, 256), F32),
            jax.ShapeDtypeStruct((ADAPTER_RANK, KEY_HEADS * HEAD_SIZE), F32),
        ),
        shares,
    )
    return (down.T, up)


def solution(mesh):
    in_specs = (
        P(("dp", "fsdp"), None),
        P(("dp", "fsdp"), None),
        P(("dp", "fsdp"), None),
        P("dp", "fsdp"),
        P("fsdp", None),
        P(),
        P(("dp", "fsdp"), None),
    )
    out_specs = (P("fsdp", None), P())
    return jax.shard_map(local, mesh=mesh, in_specs=in_specs, out_specs=out_specs, check_vma=False)
```

```python
import functools
import math

import jax
import jax.numpy as jnp
from jax import lax
from jax.experimental import pallas as pl
from jax.experimental.pallas import tpu as pltpu
from jax.sharding import PartitionSpec as P

QUERY_HEADS = 32
KEY_HEADS = 4
HEAD_SIZE = 128
ADAPTER_RANK = 64
SPAN = 8
TOKENS = 128
WINDOW = SPAN * TOKENS
N_DP = 16
N_FSDP = 32
MODEL_WIDTH = 8192
GROUP = QUERY_HEADS // KEY_HEADS
ORDER = (7, 3, 5, 1, 6, 2, 4, 0)
COST = pl.CostEstimate(flops=10**10, bytes_accessed=2**27, transcendentals=0)
BF16 = jnp.bfloat16
F32 = jnp.float32
NT = (((1,), (1,)), ((), ()))


def whole(*arrays):
    return [pl.BlockSpec(memory_space=pltpu.VMEM) for _ in arrays]


def params(mebibytes):
    return pltpu.CompilerParams(vmem_limit_bytes=mebibytes * 1024 * 1024)


def from_behind(block, distance):
    route = [(i, i + distance) for i in range(N_FSDP) if 0 <= i + distance < N_FSDP]
    return lax.ppermute(block, "fsdp", route)


def exchange(slots, axis):
    return lax.all_to_all(slots, axis, 0, 0, tiled=True)


def lowrank_kernel(weight_ref, hidden_ref, out_ref):
    total = jnp.zeros((ADAPTER_RANK, TOKENS), F32)
    for f in range(N_FSDP):
        rows = jnp.concatenate(
            [weight_ref[half, :, f * 128 : f * 128 + 128] for half in range(2)], axis=1
        )
        total += lax.dot_general(
            rows, hidden_ref[:, f * 256 : f * 256 + 256], NT, preferred_element_type=F32
        )
    out_ref[...] = total.astype(BF16)


def score_pair(query_ref, keys, bias_ref, rows, weights_ref, stats_ref, at):
    factor = math.log2(math.e) / math.sqrt(HEAD_SIZE)
    for m in range(GROUP):
        lanes = slice(m * 128, m * 128 + 128)
        scores = lax.dot_general(keys, query_ref[:, lanes], NT, preferred_element_type=F32)
        scores = scores + bias_ref[rows, :]
        top = jnp.maximum(jnp.max(scores, axis=0, keepdims=True), -1e30) * factor
        weights = jnp.exp2(scores * factor - top)
        stats_ref[at : at + 1, lanes] = top
        stats_ref[at + 1 : at + 2, lanes] = jnp.sum(weights, axis=0, keepdims=True)
        weights_ref[:, lanes] = weights.astype(BF16)


def score_kernel(
    query_ref, keys1_ref, keys0_ref, bias_ref, w1_ref, w0_ref, stats_ref
):
    for i, (keys_ref, w_ref) in enumerate(((keys1_ref, w1_ref), (keys0_ref, w0_ref))):
        rows = slice(512 + i * 256, 768 + i * 256)
        score_pair(query_ref, keys_ref[...], bias_ref, rows, w_ref, stats_ref, 2 * i)
    stats_ref[4:8, :] = jnp.zeros((4, GROUP * TOKENS), F32)


def last_score_kernel(query_ref, keys_ref, bias_ref, w3_ref, w2_ref, stats_ref):
    def key_head(g, carry):
        keys = keys_ref[:, pl.ds(pl.multiple_of(g * HEAD_SIZE, HEAD_SIZE), HEAD_SIZE)]
        lanes = pl.ds(pl.multiple_of(g * GROUP * 128, 128), GROUP * 128)
        for i, w_ref in enumerate((w3_ref, w2_ref)):
            rows = slice(i * 256, i * 256 + 256)
            score_pair(
                query_ref.at[:, lanes],
                keys[rows],
                bias_ref,
                rows,
                w_ref.at[:, lanes],
                stats_ref.at[:, lanes],
                2 * i,
            )
        return carry

    lax.fori_loop(0, KEY_HEADS, key_head, 0)


def reached_kernel(gradient_ref, up_ref, out_ref):
    def key_head(g, carry):
        up = up_ref[:, pl.ds(pl.multiple_of(g * HEAD_SIZE, HEAD_SIZE), HEAD_SIZE)]
        for m in range(GROUP):
            lanes = pl.ds(pl.multiple_of((g * GROUP + m) * 128, 128), 128)
            out_ref[:, lanes] = lax.dot_general(
                up, gradient_ref[:, lanes], NT, preferred_element_type=F32
            ).astype(BF16)
        return carry

    lax.fori_loop(0, KEY_HEADS, key_head, 0)


def sums_of(weights_ref, scale, reached):
    shares = (reached * scale).astype(BF16)
    return lax.dot_general(weights_ref[...], shares, NT, preferred_element_type=F32).T


def far_kernel(w3_ref, w2_ref, last_ref, stats_ref, reached_ref, far_ref, scale_ref):
    stats = [ref[2 * i : 2 * i + 2, :] for ref in (last_ref, stats_ref) for i in range(2)]
    top = stats[0][0:1]
    for s in stats[1:]:
        top = jnp.maximum(top, s[0:1])
    parts = [jnp.exp2(s[0:1] - top) for s in stats]
    inverse = 1.0 / sum(part * s[1:2] for part, s in zip(parts, stats))
    scales = [part * inverse for part in parts]
    for i, scale in enumerate(scales):
        scale_ref[i : i + 1, :] = scale
    reached = reached_ref[...].astype(F32)
    far_ref[:, :256] = sums_of(w3_ref, scales[0], reached).astype(BF16)
    far_ref[:, 256:] = sums_of(w2_ref, scales[1], reached).astype(BF16)


def near_kernel(w1_ref, w0_ref, scale_ref, reached_ref, near_ref):
    reached = reached_ref[...].astype(F32)
    near_ref[:, :256] = sums_of(w1_ref, scale_ref[2:3, :], reached)
    near_ref[:, 256:] = sums_of(w0_ref, scale_ref[3:4, :], reached)


def mixed_kernel(first, w3_ref, w2_ref, w1_ref, w0_ref, scale_ref, rank_ref, gradient_ref, out_ref):
    for g in range(2):
        share = jnp.zeros((ADAPTER_RANK, HEAD_SIZE), F32)
        for m in range(QUERY_HEADS // KEY_HEADS):
            h = (first + g) * 8 + m
            lanes = slice(h * 128, h * 128 + 128)
            mixed = jnp.zeros((ADAPTER_RANK, TOKENS), F32)
            for i, ref in enumerate((w3_ref, w2_ref, w1_ref, w0_ref)):
                rank = rank_ref[:, i * 256 : i * 256 + 256]
                part = jnp.dot(rank, ref[:, lanes], preferred_element_type=F32)
                mixed += part * scale_ref[i : i + 1, lanes]
            share += jnp.dot(
                mixed.astype(BF16), gradient_ref[:, lanes], preferred_element_type=F32
            )
        out_ref[:, g * 128 : g * 128 + 128] = share


DOWN = N_FSDP * 128
LANES = DOWN + 256


def shares_kernel(key_ref, hidden_ref, up0_ref, up1_ref, out_ref):
    for f in range(N_FSDP):
        product = jnp.dot(
            key_ref[...], hidden_ref[:, f * 256 : f * 256 + 256], preferred_element_type=F32
        ).astype(BF16)
        for half in range(2):
            out_ref[half, :, f * 128 : f * 128 + 128] = product[:, half * 128 : half * 128 + 128]
    for half, up_ref in enumerate((up0_ref, up1_ref)):
        out_ref[half, :, DOWN:] = up_ref[...].astype(BF16)


def fold_dp_kernel(in_ref, out_ref):
    def total(columns):
        return sum(in_ref[d, :, columns].astype(F32) for d in range(N_DP))

    up = total(slice(DOWN, LANES)).astype(BF16)
    for f in range(N_FSDP):
        out_ref[f, :, :128] = total(slice(f * 128, f * 128 + 128)).astype(BF16)
        out_ref[f, :, 128:] = up


def fold_fsdp_kernel(in_ref, out_ref):
    total = sum(in_ref[f].astype(F32) for f in range(N_FSDP))
    for d in range(N_DP):
        out_ref[d] = total


def spread_kernel(in_ref, down_ref, up_ref):
    for half in range(2):
        for part in range(8):
            rows = slice(part * 8, part * 8 + 8)
            block = in_ref[half * 8 + part]
            down_ref[rows, half * 128 : half * 128 + 128] = block[:, :128]
            up_ref[rows, half * 256 : half * 256 + 256] = block[:, 128:]


def plain(kernel, name, out_shape, *arrays):
    return pl.pallas_call(
        kernel,
        in_specs=whole(*arrays),
        out_specs=jax.tree.map(lambda _: pl.BlockSpec(memory_space=pltpu.VMEM), out_shape),
        out_shape=out_shape,
        compiler_params=params(20),
        cost_estimate=COST,
        name=name,
    )(*arrays)


def by_steps(kernel, name, steps, out_specs, out_shape, given, scratch=()):
    return pl.pallas_call(
        kernel,
        grid=(steps,),
        in_specs=[spec for spec, _ in given],
        out_specs=out_specs,
        out_shape=out_shape,
        scratch_shapes=list(scratch),
        compiler_params=params(60),
        cost_estimate=COST,
        name=name,
    )(*[array for _, array in given])


def columns(rows, lanes, first=0):
    return pl.BlockSpec((rows, lanes), lambda g: (0, first + g))


def fixed(*shape):
    return pl.BlockSpec(shape, lambda g: (0,) * len(shape))


def local(
    hidden, queries, keys, document_numbers, adapter_down_weight, adapter_up_weight, output_gradient
):
    position = lax.axis_index("fsdp")
    member = lax.axis_index("dp")
    half, part = member // 8, member % 8

    keys4 = from_behind(keys, 4)
    weight_slice = lax.dynamic_slice(adapter_down_weight.T, (part * 8, half * 128), (8, 128))
    slot = jnp.concatenate(
        [
            weight_slice,
            document_numbers.reshape(1, TOKENS).astype(BF16),
            jnp.zeros((7, 128), BF16),
        ],
        axis=0,
    )
    slots = jnp.broadcast_to(slot[None], (N_FSDP, 16, 128))
    row_parts = exchange(slots, "fsdp")
    weight_part = row_parts[:, :8].transpose(1, 0, 2).reshape(1, 8, DOWN)
    docs = row_parts[:, 8].astype(jnp.int32)
    weight_slots = jnp.broadcast_to(weight_part, (N_DP, 8, DOWN))
    weight = exchange(weight_slots, "dp").reshape(2, ADAPTER_RANK, DOWN)
    keys4 = lax.optimization_barrier((keys4, weight_slots))[0]
    pair0 = jnp.concatenate([keys4, keys], axis=0)
    pair1 = from_behind(pair0, 2)
    quad = from_behind(jnp.concatenate([pair1, pair0], axis=0), 1)

    padded = jnp.concatenate([jnp.full((SPAN - 1, TOKENS), -1, jnp.int32), docs], axis=0)
    window_docs = lax.dynamic_slice(padded, (position, 0), (SPAN, TOKENS))
    window_docs = jnp.concatenate([window_docs[7 - d : 8 - d] for d in ORDER]).reshape(WINDOW)
    own_docs = document_numbers.reshape(TOKENS)
    key_pos = jnp.concatenate([jnp.arange(TOKENS, dtype=jnp.int32) - d * TOKENS for d in ORDER])
    visible = (window_docs[:, None] == own_docs[None, :]) & (
        key_pos[:, None] <= jnp.arange(TOKENS, dtype=jnp.int32)[None, :]
    )
    bias = jnp.where(visible, 0.0, -jnp.inf).astype(F32)
    lanes = GROUP * TOKENS
    columns_of = QUERY_HEADS * TOKENS
    queries_by, keys_by, weights_by = columns(TOKENS, lanes), columns(256, 128), columns(256, lanes)
    weights_shape = jax.ShapeDtypeStruct((2 * TOKENS, columns_of), BF16)
    w1, w0, stats = by_steps(
        score_kernel,
        "score",
        KEY_HEADS,
        [weights_by] * 2 + [columns(8, lanes)],
        [weights_shape] * 2 + [jax.ShapeDtypeStruct((8, columns_of), F32)],
        [
            (queries_by, queries),
            (keys_by, pair1),
            (keys_by, pair0),
            (fixed(WINDOW, TOKENS), bias),
        ],
    )
    reached = plain(
        reached_kernel,
        "reached",
        jax.ShapeDtypeStruct((ADAPTER_RANK, columns_of), BF16),
        output_gradient,
        lax.optimization_barrier((adapter_up_weight, stats))[0],
    )
    rank = plain(
        lowrank_kernel, "lowrank", jax.ShapeDtypeStruct((ADAPTER_RANK, TOKENS), BF16), weight, hidden
    )
    rank1 = jnp.concatenate([from_behind(rank, 4), rank], axis=1)
    quad, rank1, stats = lax.optimization_barrier((quad, rank1, stats))
    rank2 = jnp.concatenate([from_behind(rank1, 2), rank1], axis=1)
    w3, w2, last = plain(
        last_score_kernel,
        "last_score",
        (weights_shape, weights_shape, jax.ShapeDtypeStruct((4, columns_of), F32)),
        queries,
        quad,
        bias,
    )
    w3, rank2 = lax.optimization_barrier((w3, rank2))
    far, scale = plain(
        far_kernel,
        "far",
        (
            jax.ShapeDtypeStruct((ADAPTER_RANK, WINDOW // 2), BF16),
            jax.ShapeDtypeStruct((4, columns_of), F32),
        ),
        w3,
        w2,
        last,
        stats,
        reached,
    )
    near = plain(
        near_kernel,
        "near",
        jax.ShapeDtypeStruct((ADAPTER_RANK, WINDOW // 2), F32),
        w1,
        w0,
        scale,
        reached,
    )
    came = from_behind(far, -1)
    near = near + came.astype(F32)
    rank3 = jnp.concatenate([from_behind(rank2, 1), rank2], axis=1)
    came = from_behind(near[:, :256], -2)
    near = near[:, 256:] + came
    came = from_behind(near[:, :128], -4)
    ups = [
        plain(
            functools.partial(mixed_kernel, first),
            "mixed",
            jax.ShapeDtypeStruct((ADAPTER_RANK, 2 * HEAD_SIZE), F32),
            w3,
            w2,
            w1,
            w0,
            scale,
            rank3,
            output_gradient,
        )
        for first in (0, 2)
    ]
    key_grad = (near[:, 128:] + came).astype(BF16)

    shares = plain(
        shares_kernel,
        "shares",
        jax.ShapeDtypeStruct((2, ADAPTER_RANK, LANES), BF16),
        key_grad,
        hidden,
        *ups,
    )
    shares = exchange(shares.reshape(N_DP, 8, LANES), "dp")
    shares = plain(
        fold_dp_kernel, "fold_dp", jax.ShapeDtypeStruct((N_FSDP, 8, 384), BF16), shares
    )
    shares = exchange(shares, "fsdp")
    shares = plain(
        fold_fsdp_kernel, "fold_fsdp", jax.ShapeDtypeStruct((N_DP, 8, 384), F32), shares
    )
    shares = exchange(shares, "dp")
    down, up = plain(
        spread_kernel,
        "spread",
        (
            jax.ShapeDtypeStruct((ADAPTER_RANK, 256), F32),
            jax.ShapeDtypeStruct((ADAPTER_RANK, KEY_HEADS * HEAD_SIZE), F32),
        ),
        shares,
    )
    return (down.T, up)


def solution(mesh):
    in_specs = (
        P(("dp", "fsdp"), None),
        P(("dp", "fsdp"), None),
        P(("dp", "fsdp"), None),
        P("dp", "fsdp"),
        P("fsdp", None),
        P(),
        P(("dp", "fsdp"), None),
    )
    out_specs = (P("fsdp", None), P())
    return jax.shard_map(local, mesh=mesh, in_specs=in_specs, out_specs=out_specs, check_vma=False)
```

```python
import functools
import math

import jax
import jax.numpy as jnp
from jax import lax
from jax.experimental import pallas as pl
from jax.experimental.pallas import tpu as pltpu
from jax.sharding import PartitionSpec as P

QUERY_HEADS = 32
KEY_HEADS = 4
HEAD_SIZE = 128
ADAPTER_RANK = 64
SPAN = 8
TOKENS = 128
WINDOW = SPAN * TOKENS
N_DP = 16
N_FSDP = 32
MODEL_WIDTH = 8192
GROUP = QUERY_HEADS // KEY_HEADS
COST = pl.CostEstimate(flops=10**10, bytes_accessed=2**27, transcendentals=0)
BF16 = jnp.bfloat16
F32 = jnp.float32
NT = (((1,), (1,)), ((), ()))


def whole(*arrays):
    return [pl.BlockSpec(memory_space=pltpu.VMEM) for _ in arrays]


def params(mebibytes):
    return pltpu.CompilerParams(vmem_limit_bytes=mebibytes * 1024 * 1024)


def from_behind(block, distance):
    route = [(i, i + distance) for i in range(N_FSDP) if 0 <= i + distance < N_FSDP]
    return lax.ppermute(block, "fsdp", route)


def exchange(slots, axis):
    return lax.all_to_all(slots, axis, 0, 0, tiled=True)


def docs_kernel(in_ref, out_ref):
    out_ref[...] = in_ref[...]


def lowrank_kernel(weight_ref, hidden_ref, out_ref):
    total = jnp.zeros((ADAPTER_RANK, TOKENS), F32)
    for f in range(N_FSDP):
        rows = jnp.concatenate(
            [weight_ref[half, :, f * 128 : f * 128 + 128] for half in range(2)], axis=1
        )
        total += lax.dot_general(
            rows, hidden_ref[:, f * 256 : f * 256 + 256], NT, preferred_element_type=F32
        )
    out_ref[...] = total.astype(BF16)


def score_pair(query_ref, keys, bias_ref, rows, weights_ref, stats_ref, at):
    factor = math.log2(math.e) / math.sqrt(HEAD_SIZE)
    for m in range(GROUP):
        lanes = slice(m * 128, m * 128 + 128)
        scores = lax.dot_general(keys, query_ref[:, lanes], NT, preferred_element_type=F32)
        scores = scores + bias_ref[rows, :]
        top = jnp.maximum(jnp.max(scores, axis=0, keepdims=True), -1e30) * factor
        weights = jnp.exp2(scores * factor - top)
        stats_ref[at : at + 1, lanes] = top
        stats_ref[at + 1 : at + 2, lanes] = jnp.sum(weights, axis=0, keepdims=True)
        weights_ref[:, lanes] = weights.astype(BF16)


def score_kernel(
    query_ref,
    keys2_ref,
    keys1_ref,
    keys0_ref,
    bias_ref,
    w2_ref,
    w1_ref,
    w0_ref,
    stats_ref,
):
    refs = ((keys2_ref, w2_ref), (keys1_ref, w1_ref), (keys0_ref, w0_ref))
    for i, (keys_ref, w_ref) in enumerate(refs):
        rows = slice(256 + i * 256, 512 + i * 256)
        score_pair(query_ref, keys_ref[...], bias_ref, rows, w_ref, stats_ref, 2 * i)
    stats_ref[6:8, :] = jnp.zeros((2, GROUP * TOKENS), F32)


def last_score_kernel(query_ref, keys_ref, bias_ref, weights_ref, stats_ref):
    def key_head(g, carry):
        keys = keys_ref[:, pl.ds(pl.multiple_of(g * HEAD_SIZE, HEAD_SIZE), HEAD_SIZE)]
        lanes = pl.ds(pl.multiple_of(g * GROUP * 128, 128), GROUP * 128)
        score_pair(
            query_ref.at[:, lanes],
            keys,
            bias_ref,
            slice(0, 256),
            weights_ref.at[:, lanes],
            stats_ref.at[:, lanes],
            0,
        )
        return carry

    lax.fori_loop(0, KEY_HEADS, key_head, 0)


def reached_kernel(gradient_ref, up_ref, out_ref):
    def key_head(g, carry):
        up = up_ref[:, pl.ds(pl.multiple_of(g * HEAD_SIZE, HEAD_SIZE), HEAD_SIZE)]
        for m in range(GROUP):
            lanes = pl.ds(pl.multiple_of((g * GROUP + m) * 128, 128), 128)
            out_ref[:, lanes] = lax.dot_general(
                up, gradient_ref[:, lanes], NT, preferred_element_type=F32
            ).astype(BF16)
        return carry

    lax.fori_loop(0, KEY_HEADS, key_head, 0)


def sums_of(weights_ref, scale, reached):
    shares = (reached * scale).astype(BF16)
    return lax.dot_general(weights_ref[...], shares, NT, preferred_element_type=F32).T


def far_kernel(w3_ref, w2_ref, last_ref, stats_ref, reached_ref, far_ref, scale_ref):
    stats = [last_ref[...]] + [stats_ref[2 * i : 2 * i + 2, :] for i in range(3)]
    top = stats[0][0:1]
    for s in stats[1:]:
        top = jnp.maximum(top, s[0:1])
    parts = [jnp.exp2(s[0:1] - top) for s in stats]
    inverse = 1.0 / sum(part * s[1:2] for part, s in zip(parts, stats))
    scales = [part * inverse for part in parts]
    for i, scale in enumerate(scales):
        scale_ref[i : i + 1, :] = scale
    reached = reached_ref[...].astype(F32)
    far_ref[:, :256] = sums_of(w3_ref, scales[0], reached).astype(BF16)
    far_ref[:, 256:] = sums_of(w2_ref, scales[1], reached).astype(BF16)


def near_kernel(w1_ref, w0_ref, scale_ref, reached_ref, near_ref):
    reached = reached_ref[...].astype(F32)
    near_ref[:, :256] = sums_of(w1_ref, scale_ref[2:3, :], reached)
    near_ref[:, 256:] = sums_of(w0_ref, scale_ref[3:4, :], reached)


def mixed_kernel(first, w3_ref, w2_ref, w1_ref, w0_ref, scale_ref, rank_ref, gradient_ref, out_ref):
    for g in range(2):
        share = jnp.zeros((ADAPTER_RANK, HEAD_SIZE), F32)
        for m in range(QUERY_HEADS // KEY_HEADS):
            h = (first + g) * 8 + m
            lanes = slice(h * 128, h * 128 + 128)
            mixed = jnp.zeros((ADAPTER_RANK, TOKENS), F32)
            for i, ref in enumerate((w3_ref, w2_ref, w1_ref, w0_ref)):
                at = (0, 2, 1, 3)[i] * 128
                rank = jnp.concatenate(
                    [rank_ref[:, at : at + 128], rank_ref[:, 512 + at : 640 + at]], axis=1
                )
                part = jnp.dot(rank, ref[:, lanes], preferred_element_type=F32)
                mixed += part * scale_ref[i : i + 1, lanes]
            share += jnp.dot(
                mixed.astype(BF16), gradient_ref[:, lanes], preferred_element_type=F32
            )
        out_ref[:, g * 128 : g * 128 + 128] = share


DOWN = N_FSDP * 128
LANES = DOWN + 256


def shares_kernel(key_ref, hidden_ref, up0_ref, up1_ref, out_ref):
    for f in range(N_FSDP):
        product = jnp.dot(
            key_ref[...], hidden_ref[:, f * 256 : f * 256 + 256], preferred_element_type=F32
        ).astype(BF16)
        for half in range(2):
            out_ref[half, :, f * 128 : f * 128 + 128] = product[:, half * 128 : half * 128 + 128]
    for half, up_ref in enumerate((up0_ref, up1_ref)):
        out_ref[half, :, DOWN:] = up_ref[...].astype(BF16)


def fold_dp_kernel(in_ref, out_ref):
    def total(columns):
        return sum(in_ref[d, :, columns].astype(F32) for d in range(N_DP))

    up = total(slice(DOWN, LANES)).astype(BF16)
    for f in range(N_FSDP):
        out_ref[f, :, :128] = total(slice(f * 128, f * 128 + 128)).astype(BF16)
        out_ref[f, :, 128:] = up


def fold_fsdp_kernel(in_ref, out_ref):
    total = sum(in_ref[f].astype(F32) for f in range(N_FSDP))
    for d in range(N_DP):
        out_ref[d] = total


def spread_kernel(in_ref, down_ref, up_ref):
    for half in range(2):
        for part in range(8):
            rows = slice(part * 8, part * 8 + 8)
            block = in_ref[half * 8 + part]
            down_ref[rows, half * 128 : half * 128 + 128] = block[:, :128]
            up_ref[rows, half * 256 : half * 256 + 256] = block[:, 128:]


def plain(kernel, name, out_shape, *arrays):
    return pl.pallas_call(
        kernel,
        in_specs=whole(*arrays),
        out_specs=jax.tree.map(lambda _: pl.BlockSpec(memory_space=pltpu.VMEM), out_shape),
        out_shape=out_shape,
        compiler_params=params(20),
        cost_estimate=COST,
        name=name,
    )(*arrays)


def by_steps(kernel, name, steps, out_specs, out_shape, given, scratch=()):
    return pl.pallas_call(
        kernel,
        grid=(steps,),
        in_specs=[spec for spec, _ in given],
        out_specs=out_specs,
        out_shape=out_shape,
        scratch_shapes=list(scratch),
        compiler_params=params(60),
        cost_estimate=COST,
        name=name,
    )(*[array for _, array in given])


def columns(rows, lanes, first=0):
    return pl.BlockSpec((rows, lanes), lambda g: (0, first + g))


def fixed(*shape):
    return pl.BlockSpec(shape, lambda g: (0,) * len(shape))


def local(
    hidden, queries, keys, document_numbers, adapter_down_weight, adapter_up_weight, output_gradient
):
    position = lax.axis_index("fsdp")
    member = lax.axis_index("dp")
    half, part = member // 8, member % 8

    keys1, keys2, keys3 = [from_behind(keys, distance) for distance in (1, 2, 3)]
    weight_slice = lax.dynamic_slice(adapter_down_weight.T, (part * 8, half * 128), (8, 128))
    slot = jnp.concatenate(
        [
            weight_slice,
            document_numbers.reshape(1, TOKENS).astype(BF16),
            jnp.zeros((7, 128), BF16),
        ],
        axis=0,
    )
    docs_row = plain(
        docs_kernel, "docs", jax.ShapeDtypeStruct((1, TOKENS), jnp.int32), document_numbers
    )
    slots = jnp.broadcast_to(slot[None], (N_FSDP, 16, 128))
    row_parts = exchange(slots, "fsdp")
    pair0 = jnp.concatenate([keys1, keys], axis=0)
    pair1 = jnp.concatenate([keys3, keys2], axis=0)
    pair2 = from_behind(pair1, 2)
    weight_part = row_parts[:, :8].transpose(1, 0, 2).reshape(1, 8, DOWN)
    docs = row_parts[:, 8].astype(jnp.int32)
    weight_slots = jnp.broadcast_to(weight_part, (N_DP, 8, DOWN))
    weight = exchange(weight_slots, "dp").reshape(2, ADAPTER_RANK, DOWN)
    pair2 = lax.optimization_barrier((pair2, weight_slots))[0]
    pair3 = from_behind(pair2, 2)

    padded = jnp.concatenate([jnp.full((SPAN - 1, TOKENS), -1, jnp.int32), docs], axis=0)
    window_docs = lax.dynamic_slice(padded, (position, 0), (SPAN, TOKENS)).reshape(WINDOW)
    own_docs = docs_row[0]
    key_pos = jnp.arange(WINDOW, dtype=jnp.int32) - (SPAN - 1) * TOKENS
    visible = (window_docs[:, None] == own_docs[None, :]) & (
        key_pos[:, None] <= jnp.arange(TOKENS, dtype=jnp.int32)[None, :]
    )
    bias = jnp.where(visible, 0.0, -jnp.inf).astype(F32)
    lanes = GROUP * TOKENS
    columns_of = QUERY_HEADS * TOKENS
    queries_by, keys_by, weights_by = columns(TOKENS, lanes), columns(256, 128), columns(256, lanes)
    weights_shape = jax.ShapeDtypeStruct((2 * TOKENS, columns_of), BF16)
    w2, w1, w0, stats = by_steps(
        score_kernel,
        "score",
        KEY_HEADS,
        [weights_by] * 3 + [columns(8, lanes)],
        [weights_shape] * 3 + [jax.ShapeDtypeStruct((8, columns_of), F32)],
        [
            (queries_by, queries),
            (keys_by, pair2),
            (keys_by, pair1),
            (keys_by, pair0),
            (fixed(WINDOW, TOKENS), bias),
        ],
    )
    reached = plain(
        reached_kernel,
        "reached",
        jax.ShapeDtypeStruct((ADAPTER_RANK, columns_of), BF16),
        output_gradient,
        lax.optimization_barrier((adapter_up_weight, stats))[0],
    )
    rank = plain(
        lowrank_kernel, "lowrank", jax.ShapeDtypeStruct((ADAPTER_RANK, TOKENS), BF16), weight, hidden
    )
    rank1 = jnp.concatenate([from_behind(rank, 4), rank], axis=1)
    pair3, rank1, stats = lax.optimization_barrier((pair3, rank1, stats))
    rank2 = jnp.concatenate([from_behind(rank1, 2), rank1], axis=1)
    w3, last = plain(
        last_score_kernel,
        "last_score",
        (weights_shape, jax.ShapeDtypeStruct((2, columns_of), F32)),
        queries,
        pair3,
        bias,
    )
    w3, rank2 = lax.optimization_barrier((w3, rank2))
    far, scale = plain(
        far_kernel,
        "far",
        (
            jax.ShapeDtypeStruct((ADAPTER_RANK, WINDOW // 2), BF16),
            jax.ShapeDtypeStruct((4, columns_of), F32),
        ),
        w3,
        w2,
        last,
        stats,
        reached,
    )
    near = plain(
        near_kernel,
        "near",
        jax.ShapeDtypeStruct((ADAPTER_RANK, WINDOW // 2), F32),
        w1,
        w0,
        scale,
        reached,
    )
    came = from_behind(far, -4)
    near = near + came.astype(F32)
    rank3 = jnp.concatenate([from_behind(rank2, 1), rank2], axis=1)
    came = from_behind(near[:, :256], -2)
    near = near[:, 256:] + came
    came = from_behind(near[:, :128], -1)
    ups = [
        plain(
            functools.partial(mixed_kernel, first),
            "mixed",
            jax.ShapeDtypeStruct((ADAPTER_RANK, 2 * HEAD_SIZE), F32),
            w3,
            w2,
            w1,
            w0,
            scale,
            rank3,
            output_gradient,
        )
        for first in (0, 2)
    ]
    key_grad = (near[:, 128:] + came).astype(BF16)

    shares = plain(
        shares_kernel,
        "shares",
        jax.ShapeDtypeStruct((2, ADAPTER_RANK, LANES), BF16),
        key_grad,
        hidden,
        *ups,
    )
    shares = exchange(shares.reshape(N_DP, 8, LANES), "dp")
    shares = plain(
        fold_dp_kernel, "fold_dp", jax.ShapeDtypeStruct((N_FSDP, 8, 384), BF16), shares
    )
    shares = exchange(shares, "fsdp")
    shares = plain(
        fold_fsdp_kernel, "fold_fsdp", jax.ShapeDtypeStruct((N_DP, 8, 384), F32), shares
    )
    shares = exchange(shares, "dp")
    down, up = plain(
        spread_kernel,
        "spread",
        (
            jax.ShapeDtypeStruct((ADAPTER_RANK, 256), F32),
            jax.ShapeDtypeStruct((ADAPTER_RANK, KEY_HEADS * HEAD_SIZE), F32),
        ),
        shares,
    )
    return (down.T, up)


def solution(mesh):
    in_specs = (
        P(("dp", "fsdp"), None),
        P(("dp", "fsdp"), None),
        P(("dp", "fsdp"), None),
        P("dp", "fsdp"),
        P("fsdp", None),
        P(),
        P(("dp", "fsdp"), None),
    )
    out_specs = (P("fsdp", None), P())
    return jax.shard_map(local, mesh=mesh, in_specs=in_specs, out_specs=out_specs, check_vma=False)
```

```python
import functools
import math

import jax
import jax.numpy as jnp
from jax import lax
from jax.experimental import pallas as pl
from jax.experimental.pallas import tpu as pltpu
from jax.sharding import PartitionSpec as P

QUERY_HEADS = 32
KEY_HEADS = 4
HEAD_SIZE = 128
ADAPTER_RANK = 64
SPAN = 8
TOKENS = 128
WINDOW = SPAN * TOKENS
N_DP = 16
N_FSDP = 32
MODEL_WIDTH = 8192
GROUP = QUERY_HEADS // KEY_HEADS
COST = pl.CostEstimate(flops=10**10, bytes_accessed=2**27, transcendentals=0)
BF16 = jnp.bfloat16
F32 = jnp.float32
NT = (((1,), (1,)), ((), ()))


def whole(*arrays):
    return [pl.BlockSpec(memory_space=pltpu.VMEM) for _ in arrays]


def params(mebibytes):
    return pltpu.CompilerParams(vmem_limit_bytes=mebibytes * 1024 * 1024)


def from_behind(block, distance):
    route = [(i, i + distance) for i in range(N_FSDP) if 0 <= i + distance < N_FSDP]
    return lax.ppermute(block, "fsdp", route)


def exchange(slots, axis):
    return lax.all_to_all(slots, axis, 0, 0, tiled=True)


def docs_kernel(in_ref, out_ref):
    out_ref[...] = in_ref[...]


def lowrank_kernel(weight_ref, hidden_ref, out_ref):
    total = jnp.zeros((ADAPTER_RANK, TOKENS), F32)
    for f in range(N_FSDP):
        rows = jnp.concatenate(
            [weight_ref[half, :, f * 128 : f * 128 + 128] for half in range(2)], axis=1
        )
        total += lax.dot_general(
            rows, hidden_ref[:, f * 256 : f * 256 + 256], NT, preferred_element_type=F32
        )
    out_ref[...] = total.astype(BF16)


def score_pair(query_ref, keys, bias_ref, rows, weights_ref, stats_ref, at):
    factor = math.log2(math.e) / math.sqrt(HEAD_SIZE)
    for m in range(GROUP):
        lanes = slice(m * 128, m * 128 + 128)
        scores = lax.dot_general(keys, query_ref[:, lanes], NT, preferred_element_type=F32)
        scores = scores + bias_ref[rows, :]
        top = jnp.maximum(jnp.max(scores, axis=0, keepdims=True), -1e30) * factor
        weights = jnp.exp2(scores * factor - top)
        stats_ref[at : at + 1, lanes] = top
        stats_ref[at + 1 : at + 2, lanes] = jnp.sum(weights, axis=0, keepdims=True)
        weights_ref[:, lanes] = weights.astype(BF16)


def score_kernel(
    query_ref,
    keys2_ref,
    keys1_ref,
    keys0_ref,
    bias_ref,
    w2_ref,
    w1_ref,
    w0_ref,
    stats_ref,
):
    refs = ((keys2_ref, w2_ref), (keys1_ref, w1_ref), (keys0_ref, w0_ref))
    for i, (keys_ref, w_ref) in enumerate(refs):
        rows = slice(256 + i * 256, 512 + i * 256)
        score_pair(query_ref, keys_ref[...], bias_ref, rows, w_ref, stats_ref, 2 * i)
    stats_ref[6:8, :] = jnp.zeros((2, GROUP * TOKENS), F32)


def last_score_kernel(query_ref, keys_ref, bias_ref, weights_ref, stats_ref):
    def key_head(g, carry):
        keys = keys_ref[:, pl.ds(pl.multiple_of(g * HEAD_SIZE, HEAD_SIZE), HEAD_SIZE)]
        lanes = pl.ds(pl.multiple_of(g * GROUP * 128, 128), GROUP * 128)
        score_pair(
            query_ref.at[:, lanes],
            keys,
            bias_ref,
            slice(0, 256),
            weights_ref.at[:, lanes],
            stats_ref.at[:, lanes],
            0,
        )
        return carry

    lax.fori_loop(0, KEY_HEADS, key_head, 0)


def reached_kernel(gradient_ref, up_ref, out_ref):
    def key_head(g, carry):
        up = up_ref[:, pl.ds(pl.multiple_of(g * HEAD_SIZE, HEAD_SIZE), HEAD_SIZE)]
        for m in range(GROUP):
            lanes = pl.ds(pl.multiple_of((g * GROUP + m) * 128, 128), 128)
            out_ref[:, lanes] = lax.dot_general(
                up, gradient_ref[:, lanes], NT, preferred_element_type=F32
            ).astype(BF16)
        return carry

    lax.fori_loop(0, KEY_HEADS, key_head, 0)


def sums_of(weights_ref, scale, reached):
    shares = (reached * scale).astype(BF16)
    return lax.dot_general(weights_ref[...], shares, NT, preferred_element_type=F32).T


def far_kernel(w3_ref, w2_ref, last_ref, stats_ref, reached_ref, far_ref, scale_ref):
    stats = [last_ref[...]] + [stats_ref[2 * i : 2 * i + 2, :] for i in range(3)]
    top = stats[0][0:1]
    for s in stats[1:]:
        top = jnp.maximum(top, s[0:1])
    parts = [jnp.exp2(s[0:1] - top) for s in stats]
    inverse = 1.0 / sum(part * s[1:2] for part, s in zip(parts, stats))
    scales = [part * inverse for part in parts]
    for i, scale in enumerate(scales):
        scale_ref[i : i + 1, :] = scale
    reached = reached_ref[...].astype(F32)
    far_ref[:, :256] = sums_of(w3_ref, scales[0], reached).astype(BF16)
    far_ref[:, 256:] = sums_of(w2_ref, scales[1], reached).astype(BF16)


def near_kernel(w1_ref, w0_ref, scale_ref, reached_ref, near_ref):
    reached = reached_ref[...].astype(F32)
    near_ref[:, :256] = sums_of(w1_ref, scale_ref[2:3, :], reached)
    near_ref[:, 256:] = sums_of(w0_ref, scale_ref[3:4, :], reached)


def mixed_kernel(first, w3_ref, w2_ref, w1_ref, w0_ref, scale_ref, rank_ref, gradient_ref, out_ref):
    for g in range(2):
        share = jnp.zeros((ADAPTER_RANK, HEAD_SIZE), F32)
        for m in range(QUERY_HEADS // KEY_HEADS):
            h = (first + g) * 8 + m
            lanes = slice(h * 128, h * 128 + 128)
            mixed = jnp.zeros((ADAPTER_RANK, TOKENS), F32)
            for i, ref in enumerate((w3_ref, w2_ref, w1_ref, w0_ref)):
                rank = rank_ref[:, i * 256 : i * 256 + 256]
                part = jnp.dot(rank, ref[:, lanes], preferred_element_type=F32)
                mixed += part * scale_ref[i : i + 1, lanes]
            share += jnp.dot(
                mixed.astype(BF16), gradient_ref[:, lanes], preferred_element_type=F32
            )
        out_ref[:, g * 128 : g * 128 + 128] = share


DOWN = N_FSDP * 128
LANES = DOWN + 256


def shares_kernel(key_ref, hidden_ref, up0_ref, up1_ref, out_ref):
    for f in range(N_FSDP):
        product = jnp.dot(
            key_ref[...], hidden_ref[:, f * 256 : f * 256 + 256], preferred_element_type=F32
        ).astype(BF16)
        for half in range(2):
            out_ref[half, :, f * 128 : f * 128 + 128] = product[:, half * 128 : half * 128 + 128]
    for half, up_ref in enumerate((up0_ref, up1_ref)):
        out_ref[half, :, DOWN:] = up_ref[...].astype(BF16)


def fold_dp_kernel(in_ref, out_ref):
    def total(columns):
        return sum(in_ref[d, :, columns].astype(F32) for d in range(N_DP))

    up = total(slice(DOWN, LANES)).astype(BF16)
    for f in range(N_FSDP):
        out_ref[f, :, :128] = total(slice(f * 128, f * 128 + 128)).astype(BF16)
        out_ref[f, :, 128:] = up


def fold_fsdp_kernel(in_ref, out_ref):
    total = sum(in_ref[f].astype(F32) for f in range(N_FSDP))
    for d in range(N_DP):
        out_ref[d] = total


def spread_kernel(in_ref, down_ref, up_ref):
    for half in range(2):
        for part in range(8):
            rows = slice(part * 8, part * 8 + 8)
            block = in_ref[half * 8 + part]
            down_ref[rows, half * 128 : half * 128 + 128] = block[:, :128]
            up_ref[rows, half * 256 : half * 256 + 256] = block[:, 128:]


def plain(kernel, name, out_shape, *arrays):
    return pl.pallas_call(
        kernel,
        in_specs=whole(*arrays),
        out_specs=jax.tree.map(lambda _: pl.BlockSpec(memory_space=pltpu.VMEM), out_shape),
        out_shape=out_shape,
        compiler_params=params(20),
        cost_estimate=COST,
        name=name,
    )(*arrays)


def by_steps(kernel, name, steps, out_specs, out_shape, given, scratch=()):
    return pl.pallas_call(
        kernel,
        grid=(steps,),
        in_specs=[spec for spec, _ in given],
        out_specs=out_specs,
        out_shape=out_shape,
        scratch_shapes=list(scratch),
        compiler_params=params(60),
        cost_estimate=COST,
        name=name,
    )(*[array for _, array in given])


def columns(rows, lanes, first=0):
    return pl.BlockSpec((rows, lanes), lambda g: (0, first + g))


def fixed(*shape):
    return pl.BlockSpec(shape, lambda g: (0,) * len(shape))


def local(
    hidden, queries, keys, document_numbers, adapter_down_weight, adapter_up_weight, output_gradient
):
    position = lax.axis_index("fsdp")
    member = lax.axis_index("dp")
    half, part = member // 8, member % 8

    keys1, keys2, keys3 = [from_behind(keys, distance) for distance in (1, 2, 3)]
    weight_slice = lax.dynamic_slice(adapter_down_weight.T, (part * 8, half * 128), (8, 128))
    slot = jnp.concatenate(
        [
            weight_slice,
            document_numbers.reshape(1, TOKENS).astype(BF16),
            jnp.zeros((7, 128), BF16),
        ],
        axis=0,
    )
    docs_row = plain(
        docs_kernel, "docs", jax.ShapeDtypeStruct((1, TOKENS), jnp.int32), document_numbers
    )
    slots = jnp.broadcast_to(slot[None], (N_FSDP, 16, 128))
    row_parts = exchange(slots, "fsdp")
    pair0 = jnp.concatenate([keys1, keys], axis=0)
    pair1 = jnp.concatenate([keys3, keys2], axis=0)
    pair2 = from_behind(pair1, 2)
    weight_part = row_parts[:, :8].transpose(1, 0, 2).reshape(1, 8, DOWN)
    docs = row_parts[:, 8].astype(jnp.int32)
    weight_slots = jnp.broadcast_to(weight_part, (N_DP, 8, DOWN))
    weight = exchange(weight_slots, "dp").reshape(2, ADAPTER_RANK, DOWN)
    pair2 = lax.optimization_barrier((pair2, weight_slots))[0]
    pair3 = from_behind(pair2, 2)

    padded = jnp.concatenate([jnp.full((SPAN - 1, TOKENS), -1, jnp.int32), docs], axis=0)
    window_docs = lax.dynamic_slice(padded, (position, 0), (SPAN, TOKENS)).reshape(WINDOW)
    own_docs = docs_row[0]
    key_pos = jnp.arange(WINDOW, dtype=jnp.int32) - (SPAN - 1) * TOKENS
    visible = (window_docs[:, None] == own_docs[None, :]) & (
        key_pos[:, None] <= jnp.arange(TOKENS, dtype=jnp.int32)[None, :]
    )
    bias = jnp.where(visible, 0.0, -jnp.inf).astype(F32)
    lanes = GROUP * TOKENS
    columns_of = QUERY_HEADS * TOKENS
    queries_by, keys_by, weights_by = columns(TOKENS, lanes), columns(256, 128), columns(256, lanes)
    weights_shape = jax.ShapeDtypeStruct((2 * TOKENS, columns_of), BF16)
    w2, w1, w0, stats = by_steps(
        score_kernel,
        "score",
        KEY_HEADS,
        [weights_by] * 3 + [columns(8, lanes)],
        [weights_shape] * 3 + [jax.ShapeDtypeStruct((8, columns_of), F32)],
        [
            (queries_by, queries),
            (keys_by, pair2),
            (keys_by, pair1),
            (keys_by, pair0),
            (fixed(WINDOW, TOKENS), bias),
        ],
    )
    reached = plain(
        reached_kernel,
        "reached",
        jax.ShapeDtypeStruct((ADAPTER_RANK, columns_of), BF16),
        output_gradient,
        lax.optimization_barrier((adapter_up_weight, stats))[0],
    )
    rank = plain(
        lowrank_kernel, "lowrank", jax.ShapeDtypeStruct((ADAPTER_RANK, TOKENS), BF16), weight, hidden
    )
    rank1 = jnp.concatenate([from_behind(rank, 1), rank], axis=1)
    pair3, rank1, stats = lax.optimization_barrier((pair3, rank1, stats))
    rank2 = jnp.concatenate([from_behind(rank1, 2), rank1], axis=1)
    w3, last = plain(
        last_score_kernel,
        "last_score",
        (weights_shape, jax.ShapeDtypeStruct((2, columns_of), F32)),
        queries,
        pair3,
        bias,
    )
    far, scale = plain(
        far_kernel,
        "far",
        (
            jax.ShapeDtypeStruct((ADAPTER_RANK, WINDOW // 2), BF16),
            jax.ShapeDtypeStruct((4, columns_of), F32),
        ),
        w3,
        w2,
        last,
        stats,
        reached,
    )
    near = plain(
        near_kernel,
        "near",
        jax.ShapeDtypeStruct((ADAPTER_RANK, WINDOW // 2), F32),
        w1,
        w0,
        scale,
        reached,
    )
    came = from_behind(far, -4)
    near = near + came.astype(F32)
    rank3 = jnp.concatenate([from_behind(rank2, 4), rank2], axis=1)
    came = from_behind(near[:, :256], -2)
    near = near[:, 256:] + came
    came = from_behind(near[:, :128], -1)
    ups = [
        plain(
            functools.partial(mixed_kernel, first),
            "mixed",
            jax.ShapeDtypeStruct((ADAPTER_RANK, 2 * HEAD_SIZE), F32),
            w3,
            w2,
            w1,
            w0,
            scale,
            rank3,
            output_gradient,
        )
        for first in (0, 2)
    ]
    key_grad = (near[:, 128:] + came).astype(BF16)

    shares = plain(
        shares_kernel,
        "shares",
        jax.ShapeDtypeStruct((2, ADAPTER_RANK, LANES), BF16),
        key_grad,
        hidden,
        *ups,
    )
    shares = exchange(shares.reshape(N_DP, 8, LANES), "dp")
    shares = plain(
        fold_dp_kernel, "fold_dp", jax.ShapeDtypeStruct((N_FSDP, 8, 384), BF16), shares
    )
    shares = exchange(shares, "fsdp")
    shares = plain(
        fold_fsdp_kernel, "fold_fsdp", jax.ShapeDtypeStruct((N_DP, 8, 384), F32), shares
    )
    shares = exchange(shares, "dp")
    down, up = plain(
        spread_kernel,
        "spread",
        (
            jax.ShapeDtypeStruct((ADAPTER_RANK, 256), F32),
            jax.ShapeDtypeStruct((ADAPTER_RANK, KEY_HEADS * HEAD_SIZE), F32),
        ),
        shares,
    )
    return (down.T, up)


def solution(mesh):
    in_specs = (
        P(("dp", "fsdp"), None),
        P(("dp", "fsdp"), None),
        P(("dp", "fsdp"), None),
        P("dp", "fsdp"),
        P("fsdp", None),
        P(),
        P(("dp", "fsdp"), None),
    )
    out_specs = (P("fsdp", None), P())
    return jax.shard_map(local, mesh=mesh, in_specs=in_specs, out_specs=out_specs, check_vma=False)
```

```python
import functools
import math

import jax
import jax.numpy as jnp
from jax import lax
from jax.experimental import pallas as pl
from jax.experimental.pallas import tpu as pltpu
from jax.sharding import PartitionSpec as P

QUERY_HEADS = 32
KEY_HEADS = 4
HEAD_SIZE = 128
ADAPTER_RANK = 64
SPAN = 8
TOKENS = 128
WINDOW = SPAN * TOKENS
N_DP = 16
N_FSDP = 32
MODEL_WIDTH = 8192
GROUP = QUERY_HEADS // KEY_HEADS
COST = pl.CostEstimate(flops=10**10, bytes_accessed=2**27, transcendentals=0)
BF16 = jnp.bfloat16
F32 = jnp.float32
NT = (((1,), (1,)), ((), ()))


def whole(*arrays):
    return [pl.BlockSpec(memory_space=pltpu.VMEM) for _ in arrays]


def params(mebibytes):
    return pltpu.CompilerParams(vmem_limit_bytes=mebibytes * 1024 * 1024)


def from_behind(block, distance):
    route = [(i, i + distance) for i in range(N_FSDP) if 0 <= i + distance < N_FSDP]
    return lax.ppermute(block, "fsdp", route)


def exchange(slots, axis):
    return lax.all_to_all(slots, axis, 0, 0, tiled=True)


def docs_kernel(in_ref, out_ref):
    out_ref[...] = in_ref[...]


def lowrank_kernel(weight_ref, hidden_ref, out_ref):
    total = jnp.zeros((ADAPTER_RANK, TOKENS), F32)
    for f in range(N_FSDP):
        rows = jnp.concatenate(
            [weight_ref[half, :, f * 128 : f * 128 + 128] for half in range(2)], axis=1
        )
        total += lax.dot_general(
            rows, hidden_ref[:, f * 256 : f * 256 + 256], NT, preferred_element_type=F32
        )
    out_ref[...] = total.astype(BF16)


def score_pair(query_ref, keys, bias_ref, rows, weights_ref, stats_ref, at):
    factor = math.log2(math.e) / math.sqrt(HEAD_SIZE)
    for m in range(GROUP):
        lanes = slice(m * 128, m * 128 + 128)
        scores = lax.dot_general(keys, query_ref[:, lanes], NT, preferred_element_type=F32)
        scores = scores + bias_ref[rows, :]
        top = jnp.maximum(jnp.max(scores, axis=0, keepdims=True), -1e30) * factor
        weights = jnp.exp2(scores * factor - top)
        stats_ref[at : at + 1, lanes] = top
        stats_ref[at + 1 : at + 2, lanes] = jnp.sum(weights, axis=0, keepdims=True)
        weights_ref[:, lanes] = weights.astype(BF16)


def score_kernel(
    query_ref,
    keys2_ref,
    keys1_ref,
    keys0_ref,
    bias_ref,
    w2_ref,
    w1_ref,
    w0_ref,
    stats_ref,
):
    refs = ((keys2_ref, w2_ref), (keys1_ref, w1_ref), (keys0_ref, w0_ref))
    for i, (keys_ref, w_ref) in enumerate(refs):
        rows = slice(256 + i * 256, 512 + i * 256)
        score_pair(query_ref, keys_ref[...], bias_ref, rows, w_ref, stats_ref, 2 * i)
    stats_ref[6:8, :] = jnp.zeros((2, GROUP * TOKENS), F32)


def last_score_kernel(query_ref, keys_ref, bias_ref, weights_ref, stats_ref):
    def key_head(g, carry):
        keys = keys_ref[:, pl.ds(pl.multiple_of(g * HEAD_SIZE, HEAD_SIZE), HEAD_SIZE)]
        lanes = pl.ds(pl.multiple_of(g * GROUP * 128, 128), GROUP * 128)
        score_pair(
            query_ref.at[:, lanes],
            keys,
            bias_ref,
            slice(0, 256),
            weights_ref.at[:, lanes],
            stats_ref.at[:, lanes],
            0,
        )
        return carry

    lax.fori_loop(0, KEY_HEADS, key_head, 0)


def reached_kernel(gradient_ref, up_ref, out_ref):
    def key_head(g, carry):
        up = up_ref[:, pl.ds(pl.multiple_of(g * HEAD_SIZE, HEAD_SIZE), HEAD_SIZE)]
        for m in range(GROUP):
            lanes = pl.ds(pl.multiple_of((g * GROUP + m) * 128, 128), 128)
            out_ref[:, lanes] = lax.dot_general(
                up, gradient_ref[:, lanes], NT, preferred_element_type=F32
            ).astype(BF16)
        return carry

    lax.fori_loop(0, KEY_HEADS, key_head, 0)


def sums_of(weights_ref, scale, reached):
    shares = (reached * scale).astype(BF16)
    return lax.dot_general(weights_ref[...], shares, NT, preferred_element_type=F32).T


def far_kernel(w3_ref, w2_ref, last_ref, stats_ref, reached_ref, far_ref, scale_ref):
    stats = [last_ref[...]] + [stats_ref[2 * i : 2 * i + 2, :] for i in range(3)]
    top = stats[0][0:1]
    for s in stats[1:]:
        top = jnp.maximum(top, s[0:1])
    parts = [jnp.exp2(s[0:1] - top) for s in stats]
    inverse = 1.0 / sum(part * s[1:2] for part, s in zip(parts, stats))
    scales = [part * inverse for part in parts]
    for i, scale in enumerate(scales):
        scale_ref[i : i + 1, :] = scale
    reached = reached_ref[...].astype(F32)
    far_ref[:, :256] = sums_of(w3_ref, scales[0], reached).astype(BF16)
    far_ref[:, 256:] = sums_of(w2_ref, scales[1], reached).astype(BF16)


def near_kernel(w1_ref, w0_ref, scale_ref, reached_ref, near_ref):
    reached = reached_ref[...].astype(F32)
    near_ref[:, :256] = sums_of(w1_ref, scale_ref[2:3, :], reached)
    near_ref[:, 256:] = sums_of(w0_ref, scale_ref[3:4, :], reached)


def mixed_kernel(first, w3_ref, w2_ref, w1_ref, w0_ref, scale_ref, rank_ref, gradient_ref, out_ref):
    for g in range(2):
        share = jnp.zeros((ADAPTER_RANK, HEAD_SIZE), F32)
        for m in range(QUERY_HEADS // KEY_HEADS):
            h = (first + g) * 8 + m
            lanes = slice(h * 128, h * 128 + 128)
            mixed = jnp.zeros((ADAPTER_RANK, TOKENS), F32)
            for i, ref in enumerate((w3_ref, w2_ref, w1_ref, w0_ref)):
                rank = rank_ref[:, i * 256 : i * 256 + 256]
                part = jnp.dot(rank, ref[:, lanes], preferred_element_type=F32)
                mixed += part * scale_ref[i : i + 1, lanes]
            share += jnp.dot(
                mixed.astype(BF16), gradient_ref[:, lanes], preferred_element_type=F32
            )
        out_ref[:, g * 128 : g * 128 + 128] = share


DOWN = N_FSDP * 128
LANES = DOWN + 256


def shares_kernel(core_ref, key_ref, hidden_ref, up0_ref, up1_ref, own_ref, other_ref):
    for core in range(2):

        @pl.when(core_ref[0] == core)
        def _(core=core):
            halves = (own_ref, other_ref) if core == 0 else (other_ref, own_ref)
            for f in range(N_FSDP):
                product = jnp.dot(
                    key_ref[...], hidden_ref[:, f * 256 : f * 256 + 256], preferred_element_type=F32
                )
                for half, ref in enumerate(halves):
                    ref[:, f * 128 : f * 128 + 128] = product[:, half * 128 : half * 128 + 128]
            halves[0][:, DOWN:] = up0_ref[...]
            halves[1][:, DOWN:] = up1_ref[...]


def add_kernel(own_ref, other_ref, out_ref):
    for part in range(8):
        rows = slice(part * 8, part * 8 + 8)
        out_ref[part] = (own_ref[rows, :] + other_ref[rows, :]).astype(BF16)


def fold_dp_kernel(in_ref, out_ref):
    def total(columns):
        return sum(in_ref[d, :, columns].astype(F32) for d in range(N_DP // 2))

    up = total(slice(DOWN, LANES)).astype(BF16)
    for f in range(N_FSDP):
        out_ref[f, :, :128] = total(slice(f * 128, f * 128 + 128)).astype(BF16)
        out_ref[f, :, 128:] = up


def fold_fsdp_kernel(in_ref, out_ref):
    total = sum(in_ref[f].astype(F32) for f in range(N_FSDP))
    for d in range(N_DP):
        out_ref[d] = total


def spread_kernel(in_ref, down_ref, up_ref):
    for half in range(2):
        for part in range(8):
            rows = slice(part * 8, part * 8 + 8)
            block = in_ref[part * 2 + half]
            down_ref[rows, half * 128 : half * 128 + 128] = block[:, :128]
            up_ref[rows, half * 256 : half * 256 + 256] = block[:, 128:]


def plain(kernel, name, out_shape, *arrays):
    return pl.pallas_call(
        kernel,
        in_specs=whole(*arrays),
        out_specs=jax.tree.map(lambda _: pl.BlockSpec(memory_space=pltpu.VMEM), out_shape),
        out_shape=out_shape,
        compiler_params=params(20),
        cost_estimate=COST,
        name=name,
    )(*arrays)


def by_steps(kernel, name, steps, out_specs, out_shape, given, scratch=()):
    return pl.pallas_call(
        kernel,
        grid=(steps,),
        in_specs=[spec for spec, _ in given],
        out_specs=out_specs,
        out_shape=out_shape,
        scratch_shapes=list(scratch),
        compiler_params=params(60),
        cost_estimate=COST,
        name=name,
    )(*[array for _, array in given])


def columns(rows, lanes, first=0):
    return pl.BlockSpec((rows, lanes), lambda g: (0, first + g))


def fixed(*shape):
    return pl.BlockSpec(shape, lambda g: (0,) * len(shape))


def local(
    hidden, queries, keys, document_numbers, adapter_down_weight, adapter_up_weight, output_gradient
):
    position = lax.axis_index("fsdp")
    member = lax.axis_index("dp")
    half, part = member // 8, member % 8

    keys1, keys2, keys3 = [from_behind(keys, distance) for distance in (1, 2, 3)]
    weight_slice = lax.dynamic_slice(adapter_down_weight.T, (part * 8, half * 128), (8, 128))
    slot = jnp.concatenate(
        [
            weight_slice,
            document_numbers.reshape(1, TOKENS).astype(BF16),
            jnp.zeros((7, 128), BF16),
        ],
        axis=0,
    )
    docs_row = plain(
        docs_kernel, "docs", jax.ShapeDtypeStruct((1, TOKENS), jnp.int32), document_numbers
    )
    slots = jnp.broadcast_to(slot[None], (N_FSDP, 16, 128))
    row_parts = exchange(slots, "fsdp")
    pair0 = jnp.concatenate([keys1, keys], axis=0)
    pair1 = jnp.concatenate([keys3, keys2], axis=0)
    pair2 = from_behind(pair1, 2)
    weight_part = row_parts[:, :8].transpose(1, 0, 2).reshape(1, 8, DOWN)
    docs = row_parts[:, 8].astype(jnp.int32)
    weight_slots = jnp.broadcast_to(weight_part, (N_DP, 8, DOWN))
    weight = exchange(weight_slots, "dp").reshape(2, ADAPTER_RANK, DOWN)
    pair2 = lax.optimization_barrier((pair2, weight_slots))[0]
    pair3 = from_behind(pair2, 2)

    padded = jnp.concatenate([jnp.full((SPAN - 1, TOKENS), -1, jnp.int32), docs], axis=0)
    window_docs = lax.dynamic_slice(padded, (position, 0), (SPAN, TOKENS)).reshape(WINDOW)
    own_docs = docs_row[0]
    key_pos = jnp.arange(WINDOW, dtype=jnp.int32) - (SPAN - 1) * TOKENS
    visible = (window_docs[:, None] == own_docs[None, :]) & (
        key_pos[:, None] <= jnp.arange(TOKENS, dtype=jnp.int32)[None, :]
    )
    bias = jnp.where(visible, 0.0, -jnp.inf).astype(F32)
    lanes = GROUP * TOKENS
    columns_of = QUERY_HEADS * TOKENS
    queries_by, keys_by, weights_by = columns(TOKENS, lanes), columns(256, 128), columns(256, lanes)
    weights_shape = jax.ShapeDtypeStruct((2 * TOKENS, columns_of), BF16)
    w2, w1, w0, stats = by_steps(
        score_kernel,
        "score",
        KEY_HEADS,
        [weights_by] * 3 + [columns(8, lanes)],
        [weights_shape] * 3 + [jax.ShapeDtypeStruct((8, columns_of), F32)],
        [
            (queries_by, queries),
            (keys_by, pair2),
            (keys_by, pair1),
            (keys_by, pair0),
            (fixed(WINDOW, TOKENS), bias),
        ],
    )
    reached = plain(
        reached_kernel,
        "reached",
        jax.ShapeDtypeStruct((ADAPTER_RANK, columns_of), BF16),
        output_gradient,
        lax.optimization_barrier((adapter_up_weight, stats))[0],
    )
    rank = plain(
        lowrank_kernel, "lowrank", jax.ShapeDtypeStruct((ADAPTER_RANK, TOKENS), BF16), weight, hidden
    )
    rank1 = jnp.concatenate([from_behind(rank, 1), rank], axis=1)
    pair3, rank1, stats = lax.optimization_barrier((pair3, rank1, stats))
    rank2 = jnp.concatenate([from_behind(rank1, 2), rank1], axis=1)
    w3, last = plain(
        last_score_kernel,
        "last_score",
        (weights_shape, jax.ShapeDtypeStruct((2, columns_of), F32)),
        queries,
        pair3,
        bias,
    )
    w3, rank2 = lax.optimization_barrier((w3, rank2))
    far, scale = plain(
        far_kernel,
        "far",
        (
            jax.ShapeDtypeStruct((ADAPTER_RANK, WINDOW // 2), BF16),
            jax.ShapeDtypeStruct((4, columns_of), F32),
        ),
        w3,
        w2,
        last,
        stats,
        reached,
    )
    near = plain(
        near_kernel,
        "near",
        jax.ShapeDtypeStruct((ADAPTER_RANK, WINDOW // 2), F32),
        w1,
        w0,
        scale,
        reached,
    )
    came = from_behind(far, -4)
    near = near + came.astype(F32)
    rank3 = jnp.concatenate([from_behind(rank2, 4), rank2], axis=1)
    came = from_behind(near[:, :256], -2)
    near = near[:, 256:] + came
    came = from_behind(near[:, :128], -1)
    ups = [
        plain(
            functools.partial(mixed_kernel, first),
            "mixed",
            jax.ShapeDtypeStruct((ADAPTER_RANK, 2 * HEAD_SIZE), F32),
            w3,
            w2,
            w1,
            w0,
            scale,
            rank3,
            output_gradient,
        )
        for first in (0, 2)
    ]
    key_grad = (near[:, 128:] + came).astype(BF16)

    share = jax.ShapeDtypeStruct((ADAPTER_RANK, LANES), F32)
    own, other = pl.pallas_call(
        shares_kernel,
        in_specs=[pl.BlockSpec(memory_space=pltpu.SMEM)] + whole(key_grad, hidden, *ups),
        out_specs=whole(share, share),
        out_shape=(share, share),
        compiler_params=params(20),
        cost_estimate=COST,
        name="shares",
    )((member % 2).astype(jnp.int32).reshape(1), key_grad, hidden, *ups)
    other = lax.ppermute(other, "dp", [(d, d ^ 1) for d in range(N_DP)])
    shares = plain(
        add_kernel, "add", jax.ShapeDtypeStruct((N_DP // 2, 8, LANES), BF16), own, other
    )
    groups = [list(range(core, N_DP, 2)) for core in range(2)]
    shares = lax.all_to_all(shares, "dp", 0, 0, axis_index_groups=groups, tiled=True)
    shares = plain(
        fold_dp_kernel, "fold_dp", jax.ShapeDtypeStruct((N_FSDP, 8, 384), BF16), shares
    )
    shares = exchange(shares, "fsdp")
    shares = plain(
        fold_fsdp_kernel, "fold_fsdp", jax.ShapeDtypeStruct((N_DP, 8, 384), F32), shares
    )
    shares = exchange(shares, "dp")
    down, up = plain(
        spread_kernel,
        "spread",
        (
            jax.ShapeDtypeStruct((ADAPTER_RANK, 256), F32),
            jax.ShapeDtypeStruct((ADAPTER_RANK, KEY_HEADS * HEAD_SIZE), F32),
        ),
        shares,
    )
    return (down.T, up)


def solution(mesh):
    in_specs = (
        P(("dp", "fsdp"), None),
        P(("dp", "fsdp"), None),
        P(("dp", "fsdp"), None),
        P("dp", "fsdp"),
        P("fsdp", None),
        P(),
        P(("dp", "fsdp"), None),
    )
    out_specs = (P("fsdp", None), P())
    return jax.shard_map(local, mesh=mesh, in_specs=in_specs, out_specs=out_specs, check_vma=False)
```
